32 devices in a mesh: gx: 16 (over z, y, core), gz: 2 (over x).
Axes of the slice: x: 2, y: 2, z: 4, core: 2. Of those that a mesh axis runs over, the one named last changes fastest.
Arguments:
- strain_inc: float32 [6, 32, 256, 256], P(None, 'gx', None, 'gz'), may hold values from -2.5 to 2.5
- stress_old: float32 [6, 32, 256, 256], P(None, 'gx', None, 'gz'), may hold values from -6 to 6
- material_id: int32 [32, 256, 256], P('gx', None, 'gz'), may hold values from 0 to 7
- cohesion: float32 [8], replicated, may hold values from 1 to 4
- friction: float32 [8], replicated, may hold values from 0.05 to 0.3
- pressure: float32 [32, 256, 256], P('gx', 'gz'), may hold values from -6 to 6
- storage: float32 [32, 256, 256], P('gx', 'gz'), may hold values from 0.5 to 4
- perm_class: int32 [32, 256, 256], P('gx', 'gz'), may hold values from 0 to 15
- perm_table: float32 [16], replicated, may hold values from 0.5 to 8
Outputs:
- pressure_next: float32 [32, 256, 256], P('gx', 'gz')
- stress_next: float32 [6, 32, 256, 256], P(None, 'gx', None, 'gz')
- node_force: float32 [3, 32, 256, 256], P(None, 'gx', None, 'gz')
The draws below stay inside these ranges and needn't reach their ends.
All inputs are finite; a program needn't handle non-finite values.
Results may differ from the reference program's by a relative error of at most 0.00002.
Values sent between devices are 32-bit elements; how exact they have to be, the bound alone decides.
A program may use at most 64 MiB of HBM per device.

```python
import math
import jax
import jax.numpy as jnp

NY = 256
NPERM = 16
NMAT = 8
NX = 32
NZ = 256


def plant(entries, stream_key, smallest, top_value):
    index_at = [jax.random.randint(jax.random.fold_in(stream_key, axis), (), 0, length) for axis, length in enumerate(entries.shape)]
    longest = entries.shape.index(max(entries.shape))
    neighbour = index_at[:longest] + [(index_at[longest] + 1) % entries.shape[longest]] + index_at[longest + 1:]
    return entries.at[tuple(index_at)].set(smallest).at[tuple(neighbour)].set(top_value)


def block_levels(rng, extent, shards, low, largest):
    def one(position, shards_of):
        steps = jax.random.uniform(jax.random.fold_in(jax.random.fold_in(rng, 6), position), (shards_of,), jnp.float32, low / len(shards), largest / len(shards))
        return jnp.repeat(jnp.exp(steps), extent[position] // shards_of).reshape((-1,) + (1,) * (len(extent) - position - 1))

    factor_of = one(*shards[0])
    for cut in shards[1:]:
        factor_of = factor_of * one(*cut)
    return factor_of


def scatter_about(stream_key, extent, deviation, reach, shards=(), dtype=jnp.bfloat16):
    drawn = jax.random.normal(stream_key, extent, jnp.float32) * deviation
    if len(shards) > 0:
        drawn = block_levels(stream_key, extent, shards, -0.22, 0.18) * drawn
    return jnp.clip(drawn, min=-reach, max=reach).astype(dtype)


def setup_inputs(seed: int = 0) -> dict:
    splits = jax.random.split(jax.random.key(seed), 10)
    strain_inc = scatter_about(splits[0], (6, NX, NY, NZ), 0.3, 2.5, ((1, 16), (3, 2)), jnp.float32)
    stress_old = scatter_about(splits[1], (6, NX, NY, NZ), 1.0, 6.0, ((1, 16), (3, 2)), jnp.float32)
    material_id = plant(jax.random.randint(splits[2], (NX, NY, NZ), 0, NMAT), jax.random.fold_in(splits[2], 1), 0, NMAT - 1).astype(jnp.int32)
    cohesion = jnp.clip(jnp.exp(jax.random.uniform(splits[3], (NMAT,), jnp.float32, math.log(1.0), math.log(4.0))), 1.0, 4.0)
    friction = jnp.clip(jax.random.uniform(splits[4], (NMAT,), jnp.float32, 0.05, 0.3), 0.05, 0.3)
    pressure = scatter_about(splits[5], (NX, NY, NZ), 1.0, 6.0, ((0, 16), (1, 2)), jnp.float32)
    storage = jnp.clip(jnp.exp(math.log(4.0) - 2.0794415 * jax.random.uniform(splits[6], (NX, NY, NZ), jnp.float32) ** block_levels(splits[6], (NX, NY, NZ), ((0, 16), (1, 2)), -0.2, 0.2)), 0.5, 4.0)
    perm_class = plant(jax.random.randint(splits[7], (NX, NY, NZ), 0, NPERM), jax.random.fold_in(splits[7], 1), 0, NPERM - 1).astype(jnp.int32)
    perm_table = jnp.clip(jnp.exp(jax.random.uniform(splits[8], (NPERM,), jnp.float32, math.log(0.5), math.log(8.0))), 0.5, 8.0)
    return {"strain_inc": strain_inc, "stress_old": stress_old, "material_id": material_id, "cohesion": cohesion, "friction": friction, "pressure": pressure, "storage": storage, "perm_class": perm_class, "perm_table": perm_table}


BIOT = 0.8
SHEAR = 1.0
BULK = 1.5
FLOOR = 0.25

def lookup(ids, table):
    result = jnp.zeros(ids.shape, jnp.float32)
    for entry in range(table.shape[0]):
        result = result + jnp.where(ids == entry, table[entry], jnp.zeros((), jnp.float32))
    return result

def neighbours():
    inner = slice(1, -1)
    return [(slice(2, None), inner, inner), (slice(0, -2), inner, inner), (inner, slice(2, None), inner), (inner, slice(0, -2), inner), (inner, inner, slice(2, None)), (inner, inner, slice(0, -2))]

def relax_sweep(pressure, conduct, storage, source):
    pressure_pad = jnp.pad(pressure, 1)
    cond_pad = jnp.pad(conduct, 1)
    numerator = source
    denominator = storage
    for offset in neighbours():
        cond_near = cond_pad[offset]
        transmit = 2.0 * conduct * cond_near / (conduct + cond_near)
        numerator = numerator + transmit * pressure_pad[offset]
        denominator = denominator + transmit
    return numerator / denominator

def plastic(strain_inc, stress_old, material_id, cohesion, friction):
    normal_mask = jnp.array([1.0, 1.0, 1.0, 0.0, 0.0, 0.0], jnp.float32).reshape(6, 1, 1, 1)
    volume = strain_inc[0] + strain_inc[1] + strain_inc[2]
    trial_stress = stress_old + 2.0 * SHEAR * (strain_inc - normal_mask * (volume / 3.0)) + BULK * volume * normal_mask
    first_invariant = trial_stress[0] + trial_stress[1] + trial_stress[2]
    deviator = trial_stress - normal_mask * (first_invariant / 3.0)
    second_invariant = 0.5 * (deviator[0] * deviator[0] + deviator[1] * deviator[1] + deviator[2] * deviator[2])
    second_invariant = second_invariant + deviator[3] * deviator[3] + deviator[4] * deviator[4] + deviator[5] * deviator[5]
    equiv_shear = jnp.sqrt(second_invariant)
    strength = lookup(material_id, cohesion)
    slope = lookup(material_id, friction)
    yield_value = equiv_shear + slope * first_invariant - strength
    multiplier = jnp.maximum(yield_value, 0.0) / (SHEAR + 9.0 * BULK * slope * slope)
    shrink_factor = jnp.maximum(1.0 - SHEAR * multiplier / jnp.maximum(equiv_shear, FLOOR), 0.0)
    new_invariant = first_invariant - 9.0 * BULK * slope * multiplier
    return deviator * shrink_factor + normal_mask * (new_invariant / 3.0)

def corner_terms(stress_next, pressure_block):
    normal_mask = jnp.array([1.0, 1.0, 1.0, 0.0, 0.0, 0.0], jnp.float32).reshape(6, 1, 1, 1)
    total = stress_next - BIOT * pressure_block * normal_mask
    col_x = jnp.stack([total[0], total[3], total[5]])
    col_y = jnp.stack([total[3], total[1], total[4]])
    col_z = jnp.stack([total[5], total[4], total[2]])
    return (col_x, col_y, col_z)

def place_corner(term, along_x, along_y):
    placed = jnp.pad(term, ((0, 0), (along_x, 1 - along_x), (0, 0), (0, 0)))
    if along_y == 1:
        placed = jnp.pad(placed, ((0, 0), (0, 0), (1, 0), (0, 0)))[:, :, :-1]
    return placed

def node_parts(col_x, col_y, col_z):
    lower = None
    upper = None
    for corner in range(8):
        along_x = corner & 1
        along_y = corner >> 1 & 1
        along_z = corner >> 2
        term = 0.25 * ((2 * along_x - 1) * col_x + (2 * along_y - 1) * col_y + (2 * along_z - 1) * col_z)
        placed = place_corner(term, along_x, along_y)
        if along_z == 0:
            lower = placed if lower is None else lower + placed
        else:
            upper = placed if upper is None else upper + placed
    node_main = lower + jnp.pad(upper[..., :-1], ((0, 0), (0, 0), (0, 0), (1, 0)))
    node_rim = upper[..., -1]
    return (node_main, node_rim)

def reference(strain_inc, stress_old, material_id, cohesion, friction, pressure, storage, perm_class, perm_table):
    strain_rate = strain_inc[0] + strain_inc[1] + strain_inc[2]
    conduct = lookup(perm_class, perm_table)
    source = storage * pressure - BIOT * strain_rate
    first_sweep = relax_sweep(pressure, conduct, storage, source)
    pressure_next = relax_sweep(first_sweep, conduct, storage, source)
    stress_next = plastic(strain_inc, stress_old, material_id, cohesion, friction)
    col_x, col_y, col_z = corner_terms(stress_next, pressure_next)
    node_main, node_rim = node_parts(col_x, col_y, col_z)
    node_force = node_main[:, :-1]
    return (pressure_next, stress_next, node_force)
```

```python
import functools

import jax
import jax.numpy as jnp
from jax import lax
from jax.experimental import pallas as pl
from jax.experimental.pallas import tpu as pltpu
from jax.sharding import PartitionSpec as P

MESH = pl.DeviceIdType.MESH
LANES = 128
PAD = 8
ROWS = 8
F32 = jnp.float32


def pick(ids, tables):
    levels = [list(t) for t in tables]
    bit = 1
    while len(levels[0]) > 1:
        odd = (ids & bit) != 0
        levels = [
            [jnp.where(odd, t[2 * j + 1], t[2 * j]) for j in range(len(t) // 2)] for t in levels
        ]
        bit *= 2
    return levels


def kernel(
    n,
    count,
    e_hbm,
    s_hbm,
    m_hbm,
    coh,
    fri,
    p_hbm,
    st_hbm,
    c_hbm,
    ptab,
    pn_hbm,
    so_hbm,
    f_hbm,
    E,
    S,
    M,
    SR,
    RF,
    PK,
    C,
    ST,
    HX,
    F1,
    HF,
    CO,
    CX,
    PN,
    EP,
    PM,
    EM,
    T,
    FS,
    SL,
    SLR,
    RM,
    RMR,
    OUTP,
    loc,
    snd,
    rcv,
):
    g = lax.axis_index("gx")
    h = lax.axis_index("gz")
    ym = SR.shape[1]
    ny = RF.shape[2]
    sem_at = [0, 0]
    rows_of = lambda who: pl.ds(pl.multiple_of(who * ny, 8), ny)
    prow_of = lambda who: pl.ds(pl.multiple_of(PAD + who * ny, 8), ny)

    def local(src, dst):
        k = sem_at[0]
        sem_at[0] += 1
        return pltpu.make_async_copy(src, dst, loc.at[k])

    def remote(src, dst, gx, gz):
        k = sem_at[1]
        sem_at[1] += 1
        return pltpu.make_async_remote_copy(
            src_ref=src,
            dst_ref=dst,
            send_sem=snd.at[k],
            recv_sem=rcv.at[k],
            device_id=(gx, gz),
            device_id_type=MESH,
        )

    has_lo, has_hi = g > 0, g < count - 1
    ld_p = [local(p_hbm.at[:, :, pl.ds(c * LANES, LANES)], PK.at[0, c, :, pl.ds(PAD, ny)]) for c in range(n)]
    ld_c = [local(c_hbm.at[:, :, pl.ds(c * LANES, LANES)], C.at[c]) for c in range(n)]
    ld_e = local(e_hbm.at[pl.ds(0, 3)], E.at[pl.ds(0, 3)])
    ld_e2 = local(e_hbm.at[pl.ds(3, 3)], E.at[pl.ds(3, 3)])
    ld_s = local(s_hbm, S)
    ld_m = local(m_hbm, M)
    ld_st = [local(st_hbm.at[:, :, pl.ds(c * LANES, LANES)], ST.at[c]) for c in range(n)]
    for cp in [ld_e] + ld_c + ld_p + [ld_m, ld_e2, ld_s] + ld_st:
        cp.start()

    PK[:, :, :, 0:PAD, :] = jnp.zeros((2, n, 2, PAD, LANES), F32)
    PK[:, :, :, PAD + ny : 2 * PAD + ny, :] = jnp.zeros((2, n, 2, PAD, LANES), F32)
    F1[:, :, 0:PAD, :] = jnp.zeros((n, 2, PAD, LANES), F32)
    F1[:, :, PAD + ny : 2 * PAD + ny, :] = jnp.zeros((n, 2, PAD, LANES), F32)

    @pl.when(jnp.logical_not(has_lo))
    def _():
        HX[0] = jnp.zeros(HX.shape[1:], F32)
        HF[0] = jnp.zeros(HF.shape[1:], F32)
        PM[0] = jnp.zeros(PM.shape[1:], F32)
        EM[0] = jnp.zeros(EM.shape[1:], F32)
        SLR[...] = jnp.zeros(SLR.shape, F32)

    @pl.when(jnp.logical_not(has_hi))
    def _():
        HX[1] = jnp.zeros(HX.shape[1:], F32)
        HF[1] = jnp.zeros(HF.shape[1:], F32)

    @pl.when(h == 0)
    def _():
        EM[...] = jnp.zeros(EM.shape, F32)
        RMR[...] = jnp.zeros(RMR.shape, F32)

    PM[:, 0:PAD, :] = jnp.zeros((3, PAD, LANES), F32)
    EM[:, 0:PAD, :] = jnp.zeros((2, PAD, LANES), F32)
    T[:, :, 0:PAD, :] = jnp.zeros((6, 2, PAD, LANES), F32)

    barrier = pltpu.get_barrier_semaphore()
    for d in range(1, n):
        pl.semaphore_signal(barrier, inc=1, device_id=(g, lax.rem(h + d, n)), device_id_type=MESH)

    @pl.when(has_lo)
    def _():
        for d in range(n):
            pl.semaphore_signal(barrier, inc=1, device_id=(g - 1, lax.rem(h + d, n)), device_id_type=MESH)

    @pl.when(has_hi)
    def _():
        for d in range(n):
            pl.semaphore_signal(barrier, inc=1, device_id=(g + 1, lax.rem(h + d, n)), device_id_type=MESH)

    ld_e.wait()

    def rate_step(i, _):
        rows = pl.ds(pl.multiple_of(i * 16, 16), 16)
        SR[:, rows, :] = E[0, :, rows, :] + E[1, :, rows, :] + E[2, :, rows, :]
        return 0

    lax.fori_loop(0, ym // 16, rate_step, 0)
    for cp in ld_c:
        cp.wait()
    ptable = [ptab[j] for j in range(ptab.shape[0])]

    def cond_step(i, _):
        rows = pl.ds(pl.multiple_of(i * ROWS, ROWS), ROWS)
        for c in range(n):
            PK[1, c, :, pl.ds(pl.multiple_of(PAD + i * ROWS, ROWS), ROWS), :] = pick(
                C[c, :, rows, :], [ptable]
            )[0][0]
        return 0

    lax.fori_loop(0, ny // ROWS, cond_step, 0)
    for cp in ld_p:
        cp.wait()

    pl.semaphore_wait(barrier, (n - 1) + n * has_lo.astype(jnp.int32) + n * has_hi.astype(jnp.int32))

    rates = []
    for d in range(1, n):
        to = lax.rem(h + d, n)
        rates.append(remote(SR.at[:, rows_of(to), :], RF.at[h], g, to))
        rates[-1].start()
    both = pl.ds(0, 2)
    chunks = pl.ds(0, n)
    inner = pl.ds(PAD, ny)
    lo_x = remote(PK.at[both, chunks, 0, inner], HX.at[1], g - 1, h)
    hi_x = remote(PK.at[both, chunks, 1, inner], HX.at[0], g + 1, h)
    lo_y = remote(PK.at[:, :, :, pl.ds(PAD, PAD)], PK.at[:, :, :, pl.ds(PAD + ny, PAD)], g, h - 1)
    hi_y = remote(PK.at[:, :, :, pl.ds(ny, PAD)], PK.at[:, :, :, pl.ds(0, PAD)], g, h + 1)
    lo_f = remote(F1.at[chunks, 0, inner], HF.at[1], g - 1, h)
    hi_f = remote(F1.at[chunks, 1, inner], HF.at[0], g + 1, h)
    lo_fy = remote(F1.at[:, :, pl.ds(PAD, PAD)], F1.at[:, :, pl.ds(PAD + ny, PAD)], g, h - 1)
    hi_fy = remote(F1.at[:, :, pl.ds(ny, PAD)], F1.at[:, :, pl.ds(0, PAD)], g, h + 1)
    rim = remote(RM, RMR, g, h + 1)
    slab = remote(SL, SLR, g + 1, h)

    def begin(lo, hi, at, size):
        @pl.when(at > 0)
        def _():
            lo.start()

        @pl.when(at < size - 1)
        def _():
            hi.start()

    def arrive(lo, hi, at, size):
        @pl.when(at > 0)
        def _():
            hi.wait_recv()

        @pl.when(at < size - 1)
        def _():
            lo.wait_recv()

    def sent(lo, hi, at, size):
        @pl.when(at > 0)
        def _():
            lo.wait_send()

        @pl.when(at < size - 1)
        def _():
            hi.wait_send()

    begin(lo_x, hi_x, g, count)
    begin(lo_y, hi_y, h, n)
    RF[h] = SR[:, rows_of(h), :]

    ld_e2.wait()
    ld_s.wait()
    ld_m.wait()
    ctable = [coh[j] for j in range(coh.shape[0])]
    ftable = [fri[j] for j in range(fri.shape[0])]

    def plastic_step(i, _):
        rows = pl.ds(pl.multiple_of(i * ROWS, ROWS), ROWS)
        prow = pl.ds(pl.multiple_of(PAD + i * ROWS, ROWS), ROWS)
        vol = SR[:, rows, :]
        base = 1.5 * vol - 2.0 * (vol * (1.0 / 3.0))
        t = [S[c, :, rows, :] + 2.0 * E[c, :, rows, :] for c in range(6)]
        t = [t[0] + base, t[1] + base, t[2] + base] + t[3:]
        inv = t[0] + t[1] + t[2]
        third = inv * (1.0 / 3.0)
        dev = [t[0] - third, t[1] - third, t[2] - third] + t[3:]
        second = 0.5 * (dev[0] * dev[0] + dev[1] * dev[1] + dev[2] * dev[2])
        second = second + dev[3] * dev[3] + dev[4] * dev[4] + dev[5] * dev[5]
        q = jnp.sqrt(second)
        (strength,), (slope,) = pick(M[:, rows, :], [ctable, ftable])
        over = jnp.maximum(q + slope * inv - strength, 0.0)
        floor = jnp.maximum(q, 0.25)
        ratio = over / ((1.0 + 13.5 * slope * slope) * floor)
        shrink = jnp.maximum(1.0 - ratio, 0.0)
        mean = (inv - 13.5 * slope * (ratio * floor)) * (1.0 / 3.0)
        for c in range(6):
            out = dev[c] * shrink
            T[c, :, prow, :] = out + mean if c < 3 else out
        return 0

    lax.fori_loop(0, ym // ROWS, plastic_step, 0)
    st_out = local(T.at[:, :, pl.ds(PAD, ym)], so_hbm)
    st_out.start()

    lane = lax.broadcasted_iota(jnp.int32, (ROWS, LANES), 1)
    first = lane == 0
    final_lane = lane == LANES - 1
    zero = jnp.zeros((ROWS, LANES), F32)
    XC, YC, ZC = (0, 3, 5), (3, 1, 4), (5, 4, 2)

    def force_step(i, _):
        rows = pl.ds(pl.multiple_of(i * ROWS, ROWS), ROWS)
        prow = pl.ds(pl.multiple_of(PAD + i * ROWS, ROWS), ROWS)
        urow = pl.ds(PAD - 1 + i * ROWS, ROWS)
        main, side = [], []
        for a in range(2):
            s_now, d_now, s_up, d_up, r_now, r_up = [], [], [], [], [], []
            for c in range(6):
                t, u = T[c, a, prow, :], T[c, a, urow, :]
                tr, ur = pltpu.roll(t, 1, 1), pltpu.roll(u, 1, 1)
                tz, uz = jnp.where(first, 0.0, tr), jnp.where(first, 0.0, ur)
                s_now.append(t + tz)
                d_now.append(tz - t)
                s_up.append(u + uz)
                d_up.append(uz - u)
                r_now.append(tr)
                r_up.append(ur)
            line, edge = [], []
            for r in range(3):
                x, y, z = XC[r], YC[r], ZC[r]
                u_r = s_now[x] + s_up[x]
                v_r = (s_up[y] - s_now[y]) + (d_now[z] + d_up[z])
                line.append((0.25 * (v_r - u_r), 0.25 * (v_r + u_r)))
                u_r = r_now[x] + r_up[x]
                v_r = (r_up[y] - r_now[y]) + (r_now[z] + r_up[z])
                edge.append((0.25 * (v_r - u_r), 0.25 * (v_r + u_r)))
            main.append(line)
            side.append(edge)
        packed = zero
        for r in range(3):
            FS[r, 0, rows, :] = main[0][r][0]
            FS[r, 1, rows, :] = main[1][r][0] + main[0][r][1]
            SL[r, rows, :] = main[1][r][1]
            cols = [side[0][r][0], side[1][r][0] + side[0][r][1], side[1][r][1]]
            for j in range(3):
                at = 3 * j + r
                col = cols[j] if at == 0 else pltpu.roll(cols[j], at, 1)
                packed = jnp.where(lane == at, col, packed)
        RM[rows, :] = packed
        return 0

    lax.fori_loop(0, ym // ROWS, force_step, 0)

    @pl.when(h < n - 1)
    def _():
        rim.start()

    for cp in ld_st:
        cp.wait()
    for cp in rates:
        cp.wait_recv()
    arrive(lo_x, hi_x, g, count)
    arrive(lo_y, hi_y, h, n)

    def up_one(parts):
        turned = [pltpu.roll(x, LANES - 1, 1) for x in parts]
        return [jnp.where(final_lane, turned[c + 1] if c + 1 < n else 0.0, turned[c]) for c in range(n)]

    def down_one(parts):
        turned = [pltpu.roll(x, 1, 1) for x in parts]
        return [jnp.where(first, turned[c - 1] if c > 0 else 0.0, turned[c]) for c in range(n)]

    def face(a, b):
        return 2.0 * a * b / (a + b)

    def sweep_one(i, _):
        rows = pl.ds(pl.multiple_of(i * ROWS, ROWS), ROWS)
        prow = pl.ds(pl.multiple_of(PAD + i * ROWS, ROWS), ROWS)
        urow = pl.ds(PAD - 1 + i * ROWS, ROWS)
        drow = pl.ds(PAD + 1 + i * ROWS, ROWS)
        mids = []
        for a in range(2):
            k = [PK[1, c, a, prow, :] for c in range(n)]
            p = [PK[0, c, a, prow, :] for c in range(n)]
            tzp = [face(x, y) for x, y in zip(k, up_one(k))]
            tzm = down_one(tzp)
            pzp, pzm = up_one(p), down_one(p)
            for c in range(n):
                tym = face(k[c], PK[1, c, a, urow, :])
                typ = face(k[c], PK[1, c, a, drow, :])
                out = face(k[c], HX[a, 1, c, rows, :])
                if a == 0:
                    mids.append(face(k[c], PK[1, c, 1, prow, :]))
                    CX[0, c, rows, :] = mids[c]
                CX[1 + a, c, rows, :] = out
                st = ST[c, a, rows, :]
                source = st * p[c] - 0.8 * RF[c, a, rows, :]
                inverse = 1.0 / (st + out + mids[c] + tym + typ + tzm[c] + tzp[c])
                num = (
                    source
                    + out * HX[a, 0, c, rows, :]
                    + mids[c] * PK[0, c, 1 - a, prow, :]
                    + tym * PK[0, c, a, urow, :]
                    + typ * PK[0, c, a, drow, :]
                    + tzm[c] * pzm[c]
                    + tzp[c] * pzp[c]
                )
                for j, val in enumerate((tym, typ, tzm[c], tzp[c], inverse, source)):
                    CO[j, c, a, rows, :] = val
                F1[c, a, prow, :] = num * inverse
        return 0

    lax.fori_loop(0, ny // ROWS, sweep_one, 0)
    begin(lo_f, hi_f, g, count)
    begin(lo_fy, hi_fy, h, n)

    @pl.when(h > 0)
    def _():
        rim.wait_recv()

    def slab_step(i, _):
        rows = pl.ds(pl.multiple_of(i * ROWS, ROWS), ROWS)
        got = RMR[rows, :]
        for r in range(3):
            SL[r, rows, :] = SL[r, rows, :] + jnp.where(first, pltpu.roll(got, LANES - 6 - r, 1), 0.0)
        return 0

    lax.fori_loop(0, ym // ROWS, slab_step, 0)

    @pl.when(has_hi)
    def _():
        slab.start()

    arrive(lo_f, hi_f, g, count)
    arrive(lo_fy, hi_fy, h, n)

    def sweep_two(i, _):
        rows = pl.ds(pl.multiple_of(i * ROWS, ROWS), ROWS)
        prow = pl.ds(pl.multiple_of(PAD + i * ROWS, ROWS), ROWS)
        urow = pl.ds(PAD - 1 + i * ROWS, ROWS)
        drow = pl.ds(PAD + 1 + i * ROWS, ROWS)
        result = []
        for a in range(2):
            p = [F1[c, a, prow, :] for c in range(n)]
            pzp, pzm = up_one(p), down_one(p)
            line = []
            for c in range(n):
                tym, typ, tzm, tzp, inverse, source = (CO[j, c, a, rows, :] for j in range(6))
                num = (
                    source
                    + CX[1 + a, c, rows, :] * HF[a, c, rows, :]
                    + CX[0, c, rows, :] * F1[c, 1 - a, prow, :]
                    + tym * F1[c, a, urow, :]
                    + typ * F1[c, a, drow, :]
                    + tzm * pzm[c]
                    + tzp * pzp[c]
                )
                new = num * inverse
                PN[c, a, rows, :] = new
                OUTP[a, rows, pl.ds(c * LANES, LANES)] = new
                line.append(new)
            result.append(line)
        for c in range(1, n):
            left, right = pltpu.roll(result[0][c - 1], 1, 1), pltpu.roll(result[1][c - 1], 2, 1)
            EP[c, rows, :] = jnp.where(first, left, right)
        return 0

    lax.fori_loop(0, ny // ROWS, sweep_two, 0)

    mine, ahead = [], []
    for d in range(1, n):
        to = lax.rem(h + d, n)
        mine.append((to, remote(PN.at[to], PM.at[pl.ds(1, 2), prow_of(h)], g, to), remote(EP.at[to], EM.at[1, prow_of(h)], g, to)))
    for d in range(n):
        to = lax.rem(h + d, n)
        ahead.append((to, remote(PN.at[to, 1], PM.at[0, prow_of(h)], g + 1, to), remote(EP.at[to], EM.at[0, prow_of(h)], g + 1, to)))
    for to, body, brim in mine:
        body.start()

        @pl.when(to > 0)
        def _():
            brim.start()

    @pl.when(has_hi)
    def _():
        for to, body, brim in ahead:
            body.start()

            @pl.when(to > 0)
            def _():
                brim.start()

    pn_out = local(OUTP, pn_hbm)
    pn_out.start()
    PM[1:3, prow_of(h), :] = PN[h]

    @pl.when(h > 0)
    def _():
        EM[1, prow_of(h), :] = EP[h]

    @pl.when(has_lo)
    def _():
        slab.wait_recv()

    for to, body, brim in mine:
        body.wait_recv()

        @pl.when(h > 0)
        def _():
            brim.wait_recv()

    @pl.when(has_lo)
    def _():
        for to, body, brim in ahead:
            body.wait_recv()

            @pl.when(h > 0)
            def _():
                brim.wait_recv()

    def last_step(i, _):
        rows = pl.ds(pl.multiple_of(i * ROWS, ROWS), ROWS)
        prow = pl.ds(pl.multiple_of(PAD + i * ROWS, ROWS), ROWS)
        urow = pl.ds(PAD - 1 + i * ROWS, ROWS)
        got = RMR[rows, :]
        lines = []
        for j in range(3):
            parts = []
            for at in (prow, urow):
                p = PM[j, at, :]
                if j == 0:
                    edge = pltpu.roll(EM[0, at, :], LANES - 1, 1)
                elif j == 1:
                    edge = EM[1, at, :]
                else:
                    edge = pltpu.roll(EM[1, at, :], LANES - 1, 1)
                pz = jnp.where(first, edge, pltpu.roll(p, 1, 1))
                parts.append((p + pz, pz - p))
            (s0, d0), (s1, d1) = parts
            lines.append((s0 + s1, s1 - s0, d0 + d1))
        for j in range(2):
            (ss0, ds0, sd0), (ss1, ds1, sd1) = lines[j], lines[j + 1]
            pressure = (ss0 - ss1, ds0 + ds1, sd0 + sd1)
            for r in range(3):
                at = 3 * j + r
                col = got if at == 0 else pltpu.roll(got, LANES - at, 1)
                total = FS[r, j, rows, :] + jnp.where(first, col, 0.0) - 0.2 * pressure[r]
                if j == 0:
                    total = total + SLR[r, rows, :]
                FS[r, j, rows, :] = total
        return 0

    lax.fori_loop(0, ym // ROWS, last_step, 0)
    f_out = local(FS, f_hbm)
    f_out.start()

    for cp in rates:
        cp.wait_send()
    sent(lo_x, hi_x, g, count)
    sent(lo_y, hi_y, h, n)
    sent(lo_f, hi_f, g, count)
    sent(lo_fy, hi_fy, h, n)

    @pl.when(h < n - 1)
    def _():
        rim.wait_send()

    for to, body, brim in mine:
        body.wait_send()

        @pl.when(to > 0)
        def _():
            brim.wait_send()

    @pl.when(has_hi)
    def _():
        slab.wait_send()
        for to, body, brim in ahead:
            body.wait_send()

            @pl.when(to > 0)
            def _():
                brim.wait_send()

    st_out.wait()
    pn_out.wait()
    f_out.wait()


def on_device(n, count, *args):
    strain_inc, pressure = args[0], args[5]
    planes, ym = strain_inc.shape[1], strain_inc.shape[2]
    ny = pressure.shape[1]
    assert planes == 2 and strain_inc.shape[3] == LANES and pressure.shape[2] == n * LANES
    vm = lambda *shape: pltpu.VMEM(shape, F32)
    vi = lambda *shape: pltpu.VMEM(shape, jnp.int32)
    any_spec = pl.BlockSpec(memory_space=pl.ANY)
    smem = pl.BlockSpec(memory_space=pltpu.SMEM)
    loads = 3 * n + 7
    sends = (n - 1) + 10 + 2 * (n - 1) + 2 * n
    return pl.pallas_call(
        functools.partial(kernel, n, count),
        out_shape=(
            jax.ShapeDtypeStruct(pressure.shape, F32),
            jax.ShapeDtypeStruct(strain_inc.shape, F32),
            jax.ShapeDtypeStruct((3,) + strain_inc.shape[1:], F32),
        ),
        in_specs=[any_spec, any_spec, any_spec, smem, smem, any_spec, any_spec, any_spec, smem],
        out_specs=(any_spec, any_spec, any_spec),
        scratch_shapes=[
            vm(6, 2, ym, LANES),
            vm(6, 2, ym, LANES),
            vi(2, ym, LANES),
            vm(2, ym, LANES),
            vm(n, 2, ny, LANES),
            vm(2, n, 2, ny + 2 * PAD, LANES),
            vi(n, 2, ny, LANES),
            vm(n, 2, ny, LANES),
            vm(2, 2, n, ny, LANES),
            vm(n, 2, ny + 2 * PAD, LANES),
            vm(2, n, ny, LANES),
            vm(6, n, 2, ny, LANES),
            vm(3, n, ny, LANES),
            vm(n, 2, ny, LANES),
            vm(n, ny, LANES),
            vm(3, PAD + ym, LANES),
            vm(2, PAD + ym, LANES),
            vm(6, 2, PAD + ym, LANES),
            vm(3, 2, ym, LANES),
            vm(3, ym, LANES),
            vm(3, ym, LANES),
            vm(ym, LANES),
            vm(ym, LANES),
            vm(2, ny, n * LANES),
            pltpu.SemaphoreType.DMA((loads,)),
            pltpu.SemaphoreType.DMA((sends,)),
            pltpu.SemaphoreType.DMA((sends,)),
        ],
        compiler_params=pltpu.CompilerParams(
            collective_id=0, has_side_effects=True, vmem_limit_bytes=48 * 1024 * 1024
        ),
    )(*args)


def solution(mesh):
    in_specs = (
        P(None, "gx", None, "gz"),
        P(None, "gx", None, "gz"),
        P("gx", None, "gz"),
        P(),
        P(),
        P("gx", "gz", None),
        P("gx", "gz", None),
        P("gx", "gz", None),
        P(),
    )
    out_specs = (P("gx", "gz", None), P(None, "gx", None, "gz"), P(None, "gx", None, "gz"))
    return jax.shard_map(
        functools.partial(on_device, mesh.shape["gz"], mesh.shape["gx"]),
        mesh=mesh,
        in_specs=in_specs,
        out_specs=out_specs,
        check_vma=False,
    )
```

```python
import functools

import jax
import jax.numpy as jnp
from jax import lax
from jax.experimental import pallas as pl
from jax.experimental.pallas import tpu as pltpu
from jax.sharding import PartitionSpec as P

MESH = pl.DeviceIdType.MESH
LANES = 128
PAD = 8
ROWS = 8
F32 = jnp.float32


def pick(ids, tables):
    levels = [list(t) for t in tables]
    bit = 1
    while len(levels[0]) > 1:
        odd = (ids & bit) != 0
        levels = [
            [jnp.where(odd, t[2 * j + 1], t[2 * j]) for j in range(len(t) // 2)] for t in levels
        ]
        bit *= 2
    return levels


def kernel(
    n,
    count,
    e_hbm,
    s_hbm,
    m_hbm,
    coh,
    fri,
    p_hbm,
    st_hbm,
    c_hbm,
    ptab,
    pn_hbm,
    so_hbm,
    f_hbm,
    E,
    S,
    M,
    SR,
    RF,
    PK,
    C,
    ST,
    HX,
    F1,
    HF,
    CO,
    CX,
    PN,
    EP,
    ET,
    ETR,
    PM,
    EM,
    T,
    FS,
    SL,
    SLR,
    RM,
    RMR,
    RT,
    RTR,
    OUTP,
    loc,
    snd,
    rcv,
):
    g = lax.axis_index("gx")
    h = lax.axis_index("gz")
    ym = SR.shape[1]
    ny = RF.shape[2]
    sem_at = [0, 0]
    rows_of = lambda who: pl.ds(pl.multiple_of(who * ny, 8), ny)
    prow_of = lambda who: pl.ds(pl.multiple_of(PAD + who * ny, 8), ny)

    def local(src, dst):
        k = sem_at[0]
        sem_at[0] += 1
        return pltpu.make_async_copy(src, dst, loc.at[k])

    def remote(src, dst, gx, gz):
        k = sem_at[1]
        sem_at[1] += 1
        return pltpu.make_async_remote_copy(
            src_ref=src,
            dst_ref=dst,
            send_sem=snd.at[k],
            recv_sem=rcv.at[k],
            device_id=(gx, gz),
            device_id_type=MESH,
        )

    has_lo, has_hi = g > 0, g < count - 1
    ld_p = [local(p_hbm.at[:, :, pl.ds(c * LANES, LANES)], PK.at[0, c, :, pl.ds(PAD, ny)]) for c in range(n)]
    ld_c = [local(c_hbm.at[:, :, pl.ds(c * LANES, LANES)], C.at[c]) for c in range(n)]
    ld_e = local(e_hbm.at[pl.ds(0, 3)], E.at[pl.ds(0, 3)])
    ld_e2 = local(e_hbm.at[pl.ds(3, 3)], E.at[pl.ds(3, 3)])
    ld_s = local(s_hbm, S)
    ld_m = local(m_hbm, M)
    ld_st = [local(st_hbm.at[:, :, pl.ds(c * LANES, LANES)], ST.at[c]) for c in range(n)]
    for cp in [ld_e] + ld_c + ld_p + [ld_m, ld_e2, ld_s] + ld_st:
        cp.start()

    PK[:, :, :, 0:PAD, :] = jnp.zeros((2, n, 2, PAD, LANES), F32)
    PK[:, :, :, PAD + ny : 2 * PAD + ny, :] = jnp.zeros((2, n, 2, PAD, LANES), F32)
    F1[:, :, 0:PAD, :] = jnp.zeros((n, 2, PAD, LANES), F32)
    F1[:, :, PAD + ny : 2 * PAD + ny, :] = jnp.zeros((n, 2, PAD, LANES), F32)

    @pl.when(jnp.logical_not(has_lo))
    def _():
        HX[0] = jnp.zeros(HX.shape[1:], F32)
        HF[0] = jnp.zeros(HF.shape[1:], F32)
        PM[0] = jnp.zeros(PM.shape[1:], F32)
        ETR[0] = jnp.zeros(ETR.shape[1:], F32)
        SLR[...] = jnp.zeros(SLR.shape, F32)

    @pl.when(jnp.logical_not(has_hi))
    def _():
        HX[1] = jnp.zeros(HX.shape[1:], F32)
        HF[1] = jnp.zeros(HF.shape[1:], F32)

    @pl.when(h == 0)
    def _():
        ETR[...] = jnp.zeros(ETR.shape, F32)
        RTR[...] = jnp.zeros(RTR.shape, F32)

    PM[:, 0:PAD, :] = jnp.zeros((3, PAD, LANES), F32)
    EM[0:PAD, :] = jnp.zeros((PAD, LANES), F32)
    T[:, :, 0:PAD, :] = jnp.zeros((6, 2, PAD, LANES), F32)

    barrier = pltpu.get_barrier_semaphore()
    for d in range(1, n):
        pl.semaphore_signal(barrier, inc=1, device_id=(g, lax.rem(h + d, n)), device_id_type=MESH)

    @pl.when(has_lo)
    def _():
        for d in range(n):
            pl.semaphore_signal(barrier, inc=1, device_id=(g - 1, lax.rem(h + d, n)), device_id_type=MESH)

    @pl.when(has_hi)
    def _():
        for d in range(n):
            pl.semaphore_signal(barrier, inc=1, device_id=(g + 1, lax.rem(h + d, n)), device_id_type=MESH)

    ld_e.wait()

    def rate_step(i, _):
        rows = pl.ds(pl.multiple_of(i * 16, 16), 16)
        SR[:, rows, :] = E[0, :, rows, :] + E[1, :, rows, :] + E[2, :, rows, :]
        return 0

    lax.fori_loop(0, ym // 16, rate_step, 0)
    for cp in ld_c:
        cp.wait()
    ptable = [ptab[j] for j in range(ptab.shape[0])]

    def cond_step(i, _):
        rows = pl.ds(pl.multiple_of(i * ROWS, ROWS), ROWS)
        for c in range(n):
            PK[1, c, :, pl.ds(pl.multiple_of(PAD + i * ROWS, ROWS), ROWS), :] = pick(
                C[c, :, rows, :], [ptable]
            )[0][0]
        return 0

    lax.fori_loop(0, ny // ROWS, cond_step, 0)
    for cp in ld_p:
        cp.wait()

    pl.semaphore_wait(barrier, (n - 1) + n * has_lo.astype(jnp.int32) + n * has_hi.astype(jnp.int32))

    rates = []
    for d in range(1, n):
        to = lax.rem(h + d, n)
        rates.append(remote(SR.at[:, rows_of(to), :], RF.at[h], g, to))
        rates[-1].start()
    both = pl.ds(0, 2)
    chunks = pl.ds(0, n)
    inner = pl.ds(PAD, ny)
    lo_x = remote(PK.at[both, chunks, 0, inner], HX.at[1], g - 1, h)
    hi_x = remote(PK.at[both, chunks, 1, inner], HX.at[0], g + 1, h)
    lo_y = remote(PK.at[:, :, :, pl.ds(PAD, PAD)], PK.at[:, :, :, pl.ds(PAD + ny, PAD)], g, h - 1)
    hi_y = remote(PK.at[:, :, :, pl.ds(ny, PAD)], PK.at[:, :, :, pl.ds(0, PAD)], g, h + 1)
    lo_f = remote(F1.at[chunks, 0, inner], HF.at[1], g - 1, h)
    hi_f = remote(F1.at[chunks, 1, inner], HF.at[0], g + 1, h)
    lo_fy = remote(F1.at[:, :, pl.ds(PAD, PAD)], F1.at[:, :, pl.ds(PAD + ny, PAD)], g, h - 1)
    hi_fy = remote(F1.at[:, :, pl.ds(ny, PAD)], F1.at[:, :, pl.ds(0, PAD)], g, h + 1)
    rim = remote(RT, RTR, g, h + 1)
    slab = remote(SL, SLR, g + 1, h)

    def begin(lo, hi, at, size):
        @pl.when(at > 0)
        def _():
            lo.start()

        @pl.when(at < size - 1)
        def _():
            hi.start()

    def arrive(lo, hi, at, size):
        @pl.when(at > 0)
        def _():
            hi.wait_recv()

        @pl.when(at < size - 1)
        def _():
            lo.wait_recv()

    def sent(lo, hi, at, size):
        @pl.when(at > 0)
        def _():
            lo.wait_send()

        @pl.when(at < size - 1)
        def _():
            hi.wait_send()

    begin(lo_x, hi_x, g, count)
    begin(lo_y, hi_y, h, n)
    RF[h] = SR[:, rows_of(h), :]

    ld_e2.wait()
    ld_s.wait()
    ld_m.wait()
    ctable = [coh[j] for j in range(coh.shape[0])]
    ftable = [fri[j] for j in range(fri.shape[0])]

    def plastic_step(i, _):
        rows = pl.ds(pl.multiple_of(i * ROWS, ROWS), ROWS)
        prow = pl.ds(pl.multiple_of(PAD + i * ROWS, ROWS), ROWS)
        vol = SR[:, rows, :]
        base = 1.5 * vol - 2.0 * (vol * (1.0 / 3.0))
        t = [S[c, :, rows, :] + 2.0 * E[c, :, rows, :] for c in range(6)]
        t = [t[0] + base, t[1] + base, t[2] + base] + t[3:]
        inv = t[0] + t[1] + t[2]
        third = inv * (1.0 / 3.0)
        dev = [t[0] - third, t[1] - third, t[2] - third] + t[3:]
        second = 0.5 * (dev[0] * dev[0] + dev[1] * dev[1] + dev[2] * dev[2])
        second = second + dev[3] * dev[3] + dev[4] * dev[4] + dev[5] * dev[5]
        q = jnp.sqrt(second)
        (strength,), (slope,) = pick(M[:, rows, :], [ctable, ftable])
        over = jnp.maximum(q + slope * inv - strength, 0.0)
        floor = jnp.maximum(q, 0.25)
        ratio = over / ((1.0 + 13.5 * slope * slope) * floor)
        shrink = jnp.maximum(1.0 - ratio, 0.0)
        mean = (inv - 13.5 * slope * (ratio * floor)) * (1.0 / 3.0)
        for c in range(6):
            out = dev[c] * shrink
            T[c, :, prow, :] = out + mean if c < 3 else out
        return 0

    lax.fori_loop(0, ym // ROWS, plastic_step, 0)
    st_out = local(T.at[:, :, pl.ds(PAD, ym)], so_hbm)
    st_out.start()

    lane = lax.broadcasted_iota(jnp.int32, (ROWS, LANES), 1)
    first = lane == 0
    final_lane = lane == LANES - 1
    zero = jnp.zeros((ROWS, LANES), F32)
    XC, YC, ZC = (0, 3, 5), (3, 1, 4), (5, 4, 2)

    def force_step(i, _):
        rows = pl.ds(pl.multiple_of(i * ROWS, ROWS), ROWS)
        prow = pl.ds(pl.multiple_of(PAD + i * ROWS, ROWS), ROWS)
        urow = pl.ds(PAD - 1 + i * ROWS, ROWS)
        main, side = [], []
        for a in range(2):
            s_now, d_now, s_up, d_up, r_now, r_up = [], [], [], [], [], []
            for c in range(6):
                t, u = T[c, a, prow, :], T[c, a, urow, :]
                tr, ur = pltpu.roll(t, 1, 1), pltpu.roll(u, 1, 1)
                tz, uz = jnp.where(first, 0.0, tr), jnp.where(first, 0.0, ur)
                s_now.append(t + tz)
                d_now.append(tz - t)
                s_up.append(u + uz)
                d_up.append(uz - u)
                r_now.append(tr)
                r_up.append(ur)
            line, edge = [], []
            for r in range(3):
                x, y, z = XC[r], YC[r], ZC[r]
                u_r = s_now[x] + s_up[x]
                v_r = (s_up[y] - s_now[y]) + (d_now[z] + d_up[z])
                line.append((0.25 * (v_r - u_r), 0.25 * (v_r + u_r)))
                u_r = r_now[x] + r_up[x]
                v_r = (r_up[y] - r_now[y]) + (r_now[z] + r_up[z])
                edge.append((0.25 * (v_r - u_r), 0.25 * (v_r + u_r)))
            main.append(line)
            side.append(edge)
        packed = zero
        for r in range(3):
            FS[r, 0, rows, :] = main[0][r][0]
            FS[r, 1, rows, :] = main[1][r][0] + main[0][r][1]
            SL[r, rows, :] = main[1][r][1]
            cols = [side[0][r][0], side[1][r][0] + side[0][r][1], side[1][r][1]]
            for j in range(3):
                at = 3 * j + r
                col = cols[j] if at == 0 else pltpu.roll(cols[j], at, 1)
                packed = jnp.where(lane == at, col, packed)
        RM[rows, :] = packed
        return 0

    lax.fori_loop(0, ym // ROWS, force_step, 0)

    for b in range(ym // LANES):
        block = slice(b * LANES, (b + 1) * LANES)
        RT[:, block] = jnp.transpose(RM[block, :])[0:16]

    @pl.when(h < n - 1)
    def _():
        rim.start()

    for cp in ld_st:
        cp.wait()
    for cp in rates:
        cp.wait_recv()
    arrive(lo_x, hi_x, g, count)
    arrive(lo_y, hi_y, h, n)

    def up_one(parts):
        turned = [pltpu.roll(x, LANES - 1, 1) for x in parts]
        return [jnp.where(final_lane, turned[c + 1] if c + 1 < n else 0.0, turned[c]) for c in range(n)]

    def down_one(parts):
        turned = [pltpu.roll(x, 1, 1) for x in parts]
        return [jnp.where(first, turned[c - 1] if c > 0 else 0.0, turned[c]) for c in range(n)]

    def face(a, b):
        return 2.0 * a * b / (a + b)

    def sweep_one(i, _):
        rows = pl.ds(pl.multiple_of(i * ROWS, ROWS), ROWS)
        prow = pl.ds(pl.multiple_of(PAD + i * ROWS, ROWS), ROWS)
        urow = pl.ds(PAD - 1 + i * ROWS, ROWS)
        drow = pl.ds(PAD + 1 + i * ROWS, ROWS)
        mids = []
        for a in range(2):
            k = [PK[1, c, a, prow, :] for c in range(n)]
            p = [PK[0, c, a, prow, :] for c in range(n)]
            tzp = [face(x, y) for x, y in zip(k, up_one(k))]
            tzm = down_one(tzp)
            pzp, pzm = up_one(p), down_one(p)
            for c in range(n):
                tym = face(k[c], PK[1, c, a, urow, :])
                typ = face(k[c], PK[1, c, a, drow, :])
                out = face(k[c], HX[a, 1, c, rows, :])
                if a == 0:
                    mids.append(face(k[c], PK[1, c, 1, prow, :]))
                    CX[0, c, rows, :] = mids[c]
                CX[1 + a, c, rows, :] = out
                st = ST[c, a, rows, :]
                source = st * p[c] - 0.8 * RF[c, a, rows, :]
                inverse = 1.0 / (st + out + mids[c] + tym + typ + tzm[c] + tzp[c])
                num = (
                    source
                    + out * HX[a, 0, c, rows, :]
                    + mids[c] * PK[0, c, 1 - a, prow, :]
                    + tym * PK[0, c, a, urow, :]
                    + typ * PK[0, c, a, drow, :]
                    + tzm[c] * pzm[c]
                    + tzp[c] * pzp[c]
                )
                for j, val in enumerate((tym, typ, tzm[c], tzp[c], inverse, source)):
                    CO[j, c, a, rows, :] = val
                F1[c, a, prow, :] = num * inverse
        return 0

    lax.fori_loop(0, ny // ROWS, sweep_one, 0)
    begin(lo_f, hi_f, g, count)
    begin(lo_fy, hi_fy, h, n)

    @pl.when(h > 0)
    def _():
        rim.wait_recv()

    for b in range(ym // LANES):
        block = slice(b * LANES, (b + 1) * LANES)
        RMR[block, :] = jnp.transpose(
            jnp.concatenate([RTR[:, block], jnp.zeros((LANES - 16, LANES), F32)], axis=0)
        )

    def slab_step(i, _):
        rows = pl.ds(pl.multiple_of(i * ROWS, ROWS), ROWS)
        got = RMR[rows, :]
        for r in range(3):
            SL[r, rows, :] = SL[r, rows, :] + jnp.where(first, pltpu.roll(got, LANES - 6 - r, 1), 0.0)
        return 0

    lax.fori_loop(0, ym // ROWS, slab_step, 0)

    arrive(lo_f, hi_f, g, count)
    arrive(lo_fy, hi_fy, h, n)

    def sweep_two(i, _):
        rows = pl.ds(pl.multiple_of(i * ROWS, ROWS), ROWS)
        prow = pl.ds(pl.multiple_of(PAD + i * ROWS, ROWS), ROWS)
        urow = pl.ds(PAD - 1 + i * ROWS, ROWS)
        drow = pl.ds(PAD + 1 + i * ROWS, ROWS)
        result = []
        for a in range(2):
            p = [F1[c, a, prow, :] for c in range(n)]
            pzp, pzm = up_one(p), down_one(p)
            line = []
            for c in range(n):
                tym, typ, tzm, tzp, inverse, source = (CO[j, c, a, rows, :] for j in range(6))
                num = (
                    source
                    + CX[1 + a, c, rows, :] * HF[a, c, rows, :]
                    + CX[0, c, rows, :] * F1[c, 1 - a, prow, :]
                    + tym * F1[c, a, urow, :]
                    + typ * F1[c, a, drow, :]
                    + tzm * pzm[c]
                    + tzp * pzp[c]
                )
                new = num * inverse
                PN[c, a, rows, :] = new
                OUTP[a, rows, pl.ds(c * LANES, LANES)] = new
                line.append(new)
            result.append(line)
        for c in range(1, n):
            left, right = pltpu.roll(result[0][c - 1], 1, 1), pltpu.roll(result[1][c - 1], 2, 1)
            EP[c, rows, :] = jnp.where(first, left, right)
        return 0

    lax.fori_loop(0, ny // ROWS, sweep_two, 0)

    for c in range(1, n):
        cols = EP[c]
        if ny < LANES:
            cols = jnp.concatenate([cols, jnp.zeros((LANES - ny, LANES), F32)], axis=0)
        ET[c] = jnp.transpose(cols)[0:PAD]

    mine, ahead = [], []
    for d in range(1, n):
        to = lax.rem(h + d, n)
        mine.append((to, remote(PN.at[to], PM.at[pl.ds(1, 2), prow_of(h)], g, to), remote(ET.at[to], ETR.at[1, h], g, to)))
    for d in range(n):
        to = lax.rem(h + d, n)
        ahead.append((to, remote(PN.at[to, 1], PM.at[0, prow_of(h)], g + 1, to), remote(ET.at[to], ETR.at[0, h], g + 1, to)))
    for to, body, brim in mine:
        body.start()

        @pl.when(to > 0)
        def _():
            brim.start()

    @pl.when(has_hi)
    def _():
        for to, body, brim in ahead:
            body.start()

            @pl.when(to > 0)
            def _():
                brim.start()

    @pl.when(has_hi)
    def _():
        slab.start()

    pn_out = local(OUTP, pn_hbm)
    pn_out.start()
    PM[1:3, prow_of(h), :] = PN[h]

    @pl.when(h > 0)
    def _():
        ETR[1, h] = ET[h]

    @pl.when(has_lo)
    def _():
        slab.wait_recv()

    for to, body, brim in mine:
        body.wait_recv()

        @pl.when(h > 0)
        def _():
            brim.wait_recv()

    @pl.when(has_lo)
    def _():
        for to, body, brim in ahead:
            body.wait_recv()

            @pl.when(h > 0)
            def _():
                brim.wait_recv()

    for c in range(n):
        parts = [ETR[0, c], ETR[1, c], jnp.zeros((LANES - 2 * PAD, LANES), F32)]
        EM[PAD + c * ny : PAD + (c + 1) * ny, :] = jnp.transpose(
            jnp.concatenate(parts, axis=0)
        )[0:ny]

    def last_step(i, _):
        rows = pl.ds(pl.multiple_of(i * ROWS, ROWS), ROWS)
        prow = pl.ds(pl.multiple_of(PAD + i * ROWS, ROWS), ROWS)
        urow = pl.ds(PAD - 1 + i * ROWS, ROWS)
        got = RMR[rows, :]
        lines = []
        for j in range(3):
            parts = []
            for at in (prow, urow):
                p = PM[j, at, :]
                edge = pltpu.roll(EM[at, :], LANES - (1, PAD, PAD + 1)[j], 1)
                pz = jnp.where(first, edge, pltpu.roll(p, 1, 1))
                parts.append((p + pz, pz - p))
            (s0, d0), (s1, d1) = parts
            lines.append((s0 + s1, s1 - s0, d0 + d1))
        for j in range(2):
            (ss0, ds0, sd0), (ss1, ds1, sd1) = lines[j], lines[j + 1]
            pressure = (ss0 - ss1, ds0 + ds1, sd0 + sd1)
            for r in range(3):
                at = 3 * j + r
                col = got if at == 0 else pltpu.roll(got, LANES - at, 1)
                total = FS[r, j, rows, :] + jnp.where(first, col, 0.0) - 0.2 * pressure[r]
                if j == 0:
                    total = total + SLR[r, rows, :]
                FS[r, j, rows, :] = total
        return 0

    lax.fori_loop(0, ym // ROWS, last_step, 0)
    f_out = local(FS, f_hbm)
    f_out.start()

    for cp in rates:
        cp.wait_send()
    sent(lo_x, hi_x, g, count)
    sent(lo_y, hi_y, h, n)
    sent(lo_f, hi_f, g, count)
    sent(lo_fy, hi_fy, h, n)

    @pl.when(h < n - 1)
    def _():
        rim.wait_send()

    for to, body, brim in mine:
        body.wait_send()

        @pl.when(to > 0)
        def _():
            brim.wait_send()

    @pl.when(has_hi)
    def _():
        slab.wait_send()
        for to, body, brim in ahead:
            body.wait_send()

            @pl.when(to > 0)
            def _():
                brim.wait_send()

    st_out.wait()
    pn_out.wait()
    f_out.wait()


def on_device(n, count, *args):
    strain_inc, pressure = args[0], args[5]
    planes, ym = strain_inc.shape[1], strain_inc.shape[2]
    ny = pressure.shape[1]
    assert ny <= LANES and ym % LANES == 0 and planes == 2 and strain_inc.shape[3] == LANES and pressure.shape[2] == n * LANES
    vm = lambda *shape: pltpu.VMEM(shape, F32)
    vi = lambda *shape: pltpu.VMEM(shape, jnp.int32)
    any_spec = pl.BlockSpec(memory_space=pl.ANY)
    smem = pl.BlockSpec(memory_space=pltpu.SMEM)
    loads = 3 * n + 7
    sends = (n - 1) + 10 + 2 * (n - 1) + 2 * n
    return pl.pallas_call(
        functools.partial(kernel, n, count),
        out_shape=(
            jax.ShapeDtypeStruct(pressure.shape, F32),
            jax.ShapeDtypeStruct(strain_inc.shape, F32),
            jax.ShapeDtypeStruct((3,) + strain_inc.shape[1:], F32),
        ),
        in_specs=[any_spec, any_spec, any_spec, smem, smem, any_spec, any_spec, any_spec, smem],
        out_specs=(any_spec, any_spec, any_spec),
        scratch_shapes=[
            vm(6, 2, ym, LANES),
            vm(6, 2, ym, LANES),
            vi(2, ym, LANES),
            vm(2, ym, LANES),
            vm(n, 2, ny, LANES),
            vm(2, n, 2, ny + 2 * PAD, LANES),
            vi(n, 2, ny, LANES),
            vm(n, 2, ny, LANES),
            vm(2, 2, n, ny, LANES),
            vm(n, 2, ny + 2 * PAD, LANES),
            vm(2, n, ny, LANES),
            vm(6, n, 2, ny, LANES),
            vm(3, n, ny, LANES),
            vm(n, 2, ny, LANES),
            vm(n, ny, LANES),
            vm(n, PAD, LANES),
            vm(2, n, PAD, LANES),
            vm(3, PAD + ym, LANES),
            vm(PAD + ym, LANES),
            vm(6, 2, PAD + ym, LANES),
            vm(3, 2, ym, LANES),
            vm(3, ym, LANES),
            vm(3, ym, LANES),
            vm(ym, LANES),
            vm(ym, LANES),
            vm(16, ym),
            vm(16, ym),
            vm(2, ny, n * LANES),
            pltpu.SemaphoreType.DMA((loads,)),
            pltpu.SemaphoreType.DMA((sends,)),
            pltpu.SemaphoreType.DMA((sends,)),
        ],
        compiler_params=pltpu.CompilerParams(
            collective_id=0, has_side_effects=True, vmem_limit_bytes=63 * 1024 * 1024
        ),
    )(*args)


def solution(mesh):
    in_specs = (
        P(None, "gx", None, "gz"),
        P(None, "gx", None, "gz"),
        P("gx", None, "gz"),
        P(),
        P(),
        P("gx", "gz", None),
        P("gx", "gz", None),
        P("gx", "gz", None),
        P(),
    )
    out_specs = (P("gx", "gz", None), P(None, "gx", None, "gz"), P(None, "gx", None, "gz"))
    return jax.shard_map(
        functools.partial(on_device, mesh.shape["gz"], mesh.shape["gx"]),
        mesh=mesh,
        in_specs=in_specs,
        out_specs=out_specs,
        check_vma=False,
    )
```

```python
import functools

import jax
import jax.numpy as jnp
from jax import lax
from jax.experimental import pallas as pl
from jax.experimental.pallas import tpu as pltpu
from jax.sharding import PartitionSpec as P

MESH = pl.DeviceIdType.MESH
LANES = 128
PAD = 8
ROWS = 8
F32 = jnp.float32


def pick(ids, tables):
    levels = [list(t) for t in tables]
    bit = 1
    while len(levels[0]) > 1:
        odd = (ids & bit) != 0
        levels = [
            [jnp.where(odd, t[2 * j + 1], t[2 * j]) for j in range(len(t) // 2)] for t in levels
        ]
        bit *= 2
    return levels


def kernel(
    n,
    count,
    e_hbm,
    s_hbm,
    m_hbm,
    coh,
    fri,
    p_hbm,
    st_hbm,
    c_hbm,
    ptab,
    pn_hbm,
    so_hbm,
    f_hbm,
    E,
    S,
    M,
    SR,
    RF,
    PK,
    C,
    ST,
    HX,
    F1,
    HF,
    CO,
    CX,
    PN,
    EP,
    ET,
    ETR,
    PM,
    EM,
    T,
    FS,
    SL,
    SLR,
    RM,
    RMR,
    RT,
    RTR,
    OUTP,
    loc,
    snd,
    rcv,
):
    g = lax.axis_index("gx")
    h = lax.axis_index("gz")
    ym = SR.shape[1]
    ny = RF.shape[2]
    sem_at = [0, 0]
    rows_of = lambda who: pl.ds(pl.multiple_of(who * ny, 8), ny)
    prow_of = lambda who: pl.ds(pl.multiple_of(PAD + who * ny, 8), ny)

    def local(src, dst):
        k = sem_at[0]
        sem_at[0] += 1
        return pltpu.make_async_copy(src, dst, loc.at[k])

    def remote(src, dst, gx, gz):
        k = sem_at[1]
        sem_at[1] += 1
        return pltpu.make_async_remote_copy(
            src_ref=src,
            dst_ref=dst,
            send_sem=snd.at[k],
            recv_sem=rcv.at[k],
            device_id=(gx, gz),
            device_id_type=MESH,
        )

    has_lo, has_hi = g > 0, g < count - 1
    ld_p = [local(p_hbm.at[:, :, pl.ds(c * LANES, LANES)], PK.at[0, c, :, pl.ds(PAD, ny)]) for c in range(n)]
    ld_c = [local(c_hbm.at[:, :, pl.ds(c * LANES, LANES)], C.at[c]) for c in range(n)]
    ld_e = local(e_hbm.at[pl.ds(0, 3)], E.at[pl.ds(0, 3)])
    ld_e2 = local(e_hbm.at[pl.ds(3, 3)], E.at[pl.ds(3, 3)])
    ld_s = local(s_hbm, S)
    ld_m = local(m_hbm, M)
    ld_st = [local(st_hbm.at[:, :, pl.ds(c * LANES, LANES)], ST.at[c]) for c in range(n)]
    for cp in [ld_e] + ld_c + ld_p + [ld_m, ld_e2, ld_s] + ld_st:
        cp.start()

    PK[:, :, :, 0:PAD, :] = jnp.zeros((2, n, 2, PAD, LANES), F32)
    PK[:, :, :, PAD + ny : 2 * PAD + ny, :] = jnp.zeros((2, n, 2, PAD, LANES), F32)
    F1[:, :, 0:PAD, :] = jnp.zeros((n, 2, PAD, LANES), F32)
    F1[:, :, PAD + ny : 2 * PAD + ny, :] = jnp.zeros((n, 2, PAD, LANES), F32)

    @pl.when(jnp.logical_not(has_lo))
    def _():
        HX[0] = jnp.zeros(HX.shape[1:], F32)
        HF[0] = jnp.zeros(HF.shape[1:], F32)
        PM[0] = jnp.zeros(PM.shape[1:], F32)
        ETR[0] = jnp.zeros(ETR.shape[1:], F32)
        SLR[...] = jnp.zeros(SLR.shape, F32)

    @pl.when(jnp.logical_not(has_hi))
    def _():
        HX[1] = jnp.zeros(HX.shape[1:], F32)
        HF[1] = jnp.zeros(HF.shape[1:], F32)

    @pl.when(h == 0)
    def _():
        ETR[...] = jnp.zeros(ETR.shape, F32)
        RTR[...] = jnp.zeros(RTR.shape, F32)

    PM[:, 0:PAD, :] = jnp.zeros((3, PAD, LANES), F32)
    EM[0:PAD, :] = jnp.zeros((PAD, LANES), F32)
    T[:, :, 0:PAD, :] = jnp.zeros((6, 2, PAD, LANES), F32)

    barrier = pltpu.get_barrier_semaphore()
    for d in range(1, n):
        pl.semaphore_signal(barrier, inc=1, device_id=(g, lax.rem(h + d, n)), device_id_type=MESH)

    @pl.when(has_lo)
    def _():
        for d in range(n):
            pl.semaphore_signal(barrier, inc=1, device_id=(g - 1, lax.rem(h + d, n)), device_id_type=MESH)

    @pl.when(has_hi)
    def _():
        for d in range(n):
            pl.semaphore_signal(barrier, inc=1, device_id=(g + 1, lax.rem(h + d, n)), device_id_type=MESH)

    ld_e.wait()

    def rate_step(i, _):
        rows = pl.ds(pl.multiple_of(i * 16, 16), 16)
        SR[:, rows, :] = E[0, :, rows, :] + E[1, :, rows, :] + E[2, :, rows, :]
        return 0

    lax.fori_loop(0, ym // 16, rate_step, 0, unroll=4)
    for cp in ld_c:
        cp.wait()
    ptable = [ptab[j] for j in range(ptab.shape[0])]

    def cond_step(i, _):
        rows = pl.ds(pl.multiple_of(i * ROWS, ROWS), ROWS)
        for c in range(n):
            PK[1, c, :, pl.ds(pl.multiple_of(PAD + i * ROWS, ROWS), ROWS), :] = pick(
                C[c, :, rows, :], [ptable]
            )[0][0]
        return 0

    lax.fori_loop(0, ny // ROWS, cond_step, 0, unroll=4)
    for cp in ld_p:
        cp.wait()

    pl.semaphore_wait(barrier, (n - 1) + n * has_lo.astype(jnp.int32) + n * has_hi.astype(jnp.int32))

    rates = []
    for d in range(1, n):
        to = lax.rem(h + d, n)
        rates.append(remote(SR.at[:, rows_of(to), :], RF.at[h], g, to))
        rates[-1].start()
    both = pl.ds(0, 2)
    chunks = pl.ds(0, n)
    inner = pl.ds(PAD, ny)
    lo_x = remote(PK.at[both, chunks, 0, inner], HX.at[1], g - 1, h)
    hi_x = remote(PK.at[both, chunks, 1, inner], HX.at[0], g + 1, h)
    lo_y = remote(PK.at[:, :, :, pl.ds(PAD, PAD)], PK.at[:, :, :, pl.ds(PAD + ny, PAD)], g, h - 1)
    hi_y = remote(PK.at[:, :, :, pl.ds(ny, PAD)], PK.at[:, :, :, pl.ds(0, PAD)], g, h + 1)
    lo_f = remote(F1.at[chunks, 0, inner], HF.at[1], g - 1, h)
    hi_f = remote(F1.at[chunks, 1, inner], HF.at[0], g + 1, h)
    lo_fy = remote(F1.at[:, :, pl.ds(PAD, PAD)], F1.at[:, :, pl.ds(PAD + ny, PAD)], g, h - 1)
    hi_fy = remote(F1.at[:, :, pl.ds(ny, PAD)], F1.at[:, :, pl.ds(0, PAD)], g, h + 1)
    rim = remote(RT, RTR, g, h + 1)
    slab = remote(SL, SLR, g + 1, h)

    def begin(lo, hi, at, size):
        @pl.when(at > 0)
        def _():
            lo.start()

        @pl.when(at < size - 1)
        def _():
            hi.start()

    def arrive(lo, hi, at, size):
        @pl.when(at > 0)
        def _():
            hi.wait_recv()

        @pl.when(at < size - 1)
        def _():
            lo.wait_recv()

    def sent(lo, hi, at, size):
        @pl.when(at > 0)
        def _():
            lo.wait_send()

        @pl.when(at < size - 1)
        def _():
            hi.wait_send()

    begin(lo_x, hi_x, g, count)
    begin(lo_y, hi_y, h, n)
    RF[h] = SR[:, rows_of(h), :]

    ld_e2.wait()
    ld_s.wait()
    ld_m.wait()
    ctable = [coh[j] for j in range(coh.shape[0])]
    ftable = [fri[j] for j in range(fri.shape[0])]

    def plastic_step(i, _):
        rows = pl.ds(pl.multiple_of(i * ROWS, ROWS), ROWS)
        prow = pl.ds(pl.multiple_of(PAD + i * ROWS, ROWS), ROWS)
        vol = SR[:, rows, :]
        base = 1.5 * vol - 2.0 * (vol * (1.0 / 3.0))
        t = [S[c, :, rows, :] + 2.0 * E[c, :, rows, :] for c in range(6)]
        t = [t[0] + base, t[1] + base, t[2] + base] + t[3:]
        inv = t[0] + t[1] + t[2]
        third = inv * (1.0 / 3.0)
        dev = [t[0] - third, t[1] - third, t[2] - third] + t[3:]
        second = 0.5 * (dev[0] * dev[0] + dev[1] * dev[1] + dev[2] * dev[2])
        second = second + dev[3] * dev[3] + dev[4] * dev[4] + dev[5] * dev[5]
        q = jnp.sqrt(second)
        (strength,), (slope,) = pick(M[:, rows, :], [ctable, ftable])
        over = jnp.maximum(q + slope * inv - strength, 0.0)
        floor = jnp.maximum(q, 0.25)
        ratio = over / ((1.0 + 13.5 * slope * slope) * floor)
        shrink = jnp.maximum(1.0 - ratio, 0.0)
        mean = (inv - 13.5 * slope * (ratio * floor)) * (1.0 / 3.0)
        for c in range(6):
            out = dev[c] * shrink
            T[c, :, prow, :] = out + mean if c < 3 else out
        return 0

    lax.fori_loop(0, ym // ROWS, plastic_step, 0, unroll=4)
    st_out = local(T.at[:, :, pl.ds(PAD, ym)], so_hbm)
    st_out.start()

    lane = lax.broadcasted_iota(jnp.int32, (ROWS, LANES), 1)
    first = lane == 0
    final_lane = lane == LANES - 1
    zero = jnp.zeros((ROWS, LANES), F32)
    XC, YC, ZC = (0, 3, 5), (3, 1, 4), (5, 4, 2)

    def force_step(i, _):
        rows = pl.ds(pl.multiple_of(i * ROWS, ROWS), ROWS)
        prow = pl.ds(pl.multiple_of(PAD + i * ROWS, ROWS), ROWS)
        urow = pl.ds(PAD - 1 + i * ROWS, ROWS)
        main, side = [], []
        for a in range(2):
            s_now, d_now, s_up, d_up, r_now, r_up = [], [], [], [], [], []
            for c in range(6):
                t, u = T[c, a, prow, :], T[c, a, urow, :]
                tr, ur = pltpu.roll(t, 1, 1), pltpu.roll(u, 1, 1)
                tz, uz = jnp.where(first, 0.0, tr), jnp.where(first, 0.0, ur)
                s_now.append(t + tz)
                d_now.append(tz - t)
                s_up.append(u + uz)
                d_up.append(uz - u)
                r_now.append(tr)
                r_up.append(ur)
            line, edge = [], []
            for r in range(3):
                x, y, z = XC[r], YC[r], ZC[r]
                u_r = s_now[x] + s_up[x]
                v_r = (s_up[y] - s_now[y]) + (d_now[z] + d_up[z])
                line.append((0.25 * (v_r - u_r), 0.25 * (v_r + u_r)))
                u_r = r_now[x] + r_up[x]
                v_r = (r_up[y] - r_now[y]) + (r_now[z] + r_up[z])
                edge.append((0.25 * (v_r - u_r), 0.25 * (v_r + u_r)))
            main.append(line)
            side.append(edge)
        packed = zero
        for r in range(3):
            FS[r, 0, rows, :] = main[0][r][0]
            FS[r, 1, rows, :] = main[1][r][0] + main[0][r][1]
            SL[r, rows, :] = main[1][r][1]
            cols = [side[0][r][0], side[1][r][0] + side[0][r][1], side[1][r][1]]
            for j in range(3):
                at = 3 * j + r
                col = cols[j] if at == 0 else pltpu.roll(cols[j], at, 1)
                packed = jnp.where(lane == at, col, packed)
        RM[rows, :] = packed
        return 0

    lax.fori_loop(0, ym // ROWS, force_step, 0, unroll=4)

    for b in range(ym // LANES):
        block = slice(b * LANES, (b + 1) * LANES)
        RT[:, block] = jnp.transpose(RM[block, :])[0:16]

    @pl.when(h < n - 1)
    def _():
        rim.start()

    for cp in ld_st:
        cp.wait()
    for cp in rates:
        cp.wait_recv()
    arrive(lo_x, hi_x, g, count)
    arrive(lo_y, hi_y, h, n)

    def up_one(parts):
        turned = [pltpu.roll(x, LANES - 1, 1) for x in parts]
        return [jnp.where(final_lane, turned[c + 1] if c + 1 < n else 0.0, turned[c]) for c in range(n)]

    def down_one(parts):
        turned = [pltpu.roll(x, 1, 1) for x in parts]
        return [jnp.where(first, turned[c - 1] if c > 0 else 0.0, turned[c]) for c in range(n)]

    def face(a, b):
        return 2.0 * a * b / (a + b)

    def sweep_one(i, _):
        rows = pl.ds(pl.multiple_of(i * ROWS, ROWS), ROWS)
        prow = pl.ds(pl.multiple_of(PAD + i * ROWS, ROWS), ROWS)
        urow = pl.ds(PAD - 1 + i * ROWS, ROWS)
        drow = pl.ds(PAD + 1 + i * ROWS, ROWS)
        mids = []
        for a in range(2):
            k = [PK[1, c, a, prow, :] for c in range(n)]
            p = [PK[0, c, a, prow, :] for c in range(n)]
            tzp = [face(x, y) for x, y in zip(k, up_one(k))]
            tzm = down_one(tzp)
            pzp, pzm = up_one(p), down_one(p)
            for c in range(n):
                tym = face(k[c], PK[1, c, a, urow, :])
                typ = face(k[c], PK[1, c, a, drow, :])
                out = face(k[c], HX[a, 1, c, rows, :])
                if a == 0:
                    mids.append(face(k[c], PK[1, c, 1, prow, :]))
                    CX[0, c, rows, :] = mids[c]
                CX[1 + a, c, rows, :] = out
                st = ST[c, a, rows, :]
                source = st * p[c] - 0.8 * RF[c, a, rows, :]
                inverse = 1.0 / (st + out + mids[c] + tym + typ + tzm[c] + tzp[c])
                num = (
                    source
                    + out * HX[a, 0, c, rows, :]
                    + mids[c] * PK[0, c, 1 - a, prow, :]
                    + tym * PK[0, c, a, urow, :]
                    + typ * PK[0, c, a, drow, :]
                    + tzm[c] * pzm[c]
                    + tzp[c] * pzp[c]
                )
                for j, val in enumerate((tym, typ, tzm[c], tzp[c], inverse, source)):
                    CO[j, c, a, rows, :] = val
                F1[c, a, prow, :] = num * inverse
        return 0

    lax.fori_loop(0, ny // ROWS, sweep_one, 0, unroll=4)
    begin(lo_f, hi_f, g, count)
    begin(lo_fy, hi_fy, h, n)

    @pl.when(h > 0)
    def _():
        rim.wait_recv()

    for b in range(ym // LANES):
        block = slice(b * LANES, (b + 1) * LANES)
        RMR[block, :] = jnp.transpose(
            jnp.concatenate([RTR[:, block], jnp.zeros((LANES - 16, LANES), F32)], axis=0)
        )

    def slab_step(i, _):
        rows = pl.ds(pl.multiple_of(i * ROWS, ROWS), ROWS)
        got = RMR[rows, :]
        for r in range(3):
            SL[r, rows, :] = SL[r, rows, :] + jnp.where(first, pltpu.roll(got, LANES - 6 - r, 1), 0.0)
        return 0

    lax.fori_loop(0, ym // ROWS, slab_step, 0, unroll=4)

    arrive(lo_f, hi_f, g, count)
    arrive(lo_fy, hi_fy, h, n)

    def sweep_two(i, _):
        rows = pl.ds(pl.multiple_of(i * ROWS, ROWS), ROWS)
        prow = pl.ds(pl.multiple_of(PAD + i * ROWS, ROWS), ROWS)
        urow = pl.ds(PAD - 1 + i * ROWS, ROWS)
        drow = pl.ds(PAD + 1 + i * ROWS, ROWS)
        result = []
        for a in range(2):
            p = [F1[c, a, prow, :] for c in range(n)]
            pzp, pzm = up_one(p), down_one(p)
            line = []
            for c in range(n):
                tym, typ, tzm, tzp, inverse, source = (CO[j, c, a, rows, :] for j in range(6))
                num = (
                    source
                    + CX[1 + a, c, rows, :] * HF[a, c, rows, :]
                    + CX[0, c, rows, :] * F1[c, 1 - a, prow, :]
                    + tym * F1[c, a, urow, :]
                    + typ * F1[c, a, drow, :]
                    + tzm * pzm[c]
                    + tzp * pzp[c]
                )
                new = num * inverse
                PN[c, a, rows, :] = new
                OUTP[a, rows, pl.ds(c * LANES, LANES)] = new
                line.append(new)
            result.append(line)
        for c in range(1, n):
            left, right = pltpu.roll(result[0][c - 1], 1, 1), pltpu.roll(result[1][c - 1], 2, 1)
            EP[c, rows, :] = jnp.where(first, left, right)
        return 0

    lax.fori_loop(0, ny // ROWS, sweep_two, 0, unroll=4)

    for c in range(1, n):
        cols = EP[c]
        if ny < LANES:
            cols = jnp.concatenate([cols, jnp.zeros((LANES - ny, LANES), F32)], axis=0)
        ET[c] = jnp.transpose(cols)[0:PAD]

    mine, ahead = [], []
    for d in range(1, n):
        to = lax.rem(h + d, n)
        mine.append((to, remote(PN.at[to], PM.at[pl.ds(1, 2), prow_of(h)], g, to), remote(ET.at[to], ETR.at[1, h], g, to)))
    for d in range(n):
        to = lax.rem(h + d, n)
        ahead.append((to, remote(PN.at[to, 1], PM.at[0, prow_of(h)], g + 1, to), remote(ET.at[to], ETR.at[0, h], g + 1, to)))
    for to, body, brim in mine:
        body.start()

        @pl.when(to > 0)
        def _():
            brim.start()

    @pl.when(has_hi)
    def _():
        for to, body, brim in ahead:
            body.start()

            @pl.when(to > 0)
            def _():
                brim.start()

    @pl.when(has_hi)
    def _():
        slab.start()

    pn_out = local(OUTP, pn_hbm)
    pn_out.start()
    PM[1:3, prow_of(h), :] = PN[h]

    @pl.when(h > 0)
    def _():
        ETR[1, h] = ET[h]

    @pl.when(has_lo)
    def _():
        slab.wait_recv()

    for to, body, brim in mine:
        body.wait_recv()

        @pl.when(h > 0)
        def _():
            brim.wait_recv()

    @pl.when(has_lo)
    def _():
        for to, body, brim in ahead:
            body.wait_recv()

            @pl.when(h > 0)
            def _():
                brim.wait_recv()

    for c in range(n):
        parts = [ETR[0, c], ETR[1, c], jnp.zeros((LANES - 2 * PAD, LANES), F32)]
        EM[PAD + c * ny : PAD + (c + 1) * ny, :] = jnp.transpose(
            jnp.concatenate(parts, axis=0)
        )[0:ny]

    def last_step(i, _):
        rows = pl.ds(pl.multiple_of(i * ROWS, ROWS), ROWS)
        prow = pl.ds(pl.multiple_of(PAD + i * ROWS, ROWS), ROWS)
        urow = pl.ds(PAD - 1 + i * ROWS, ROWS)
        got = RMR[rows, :]
        lines = []
        for j in range(3):
            parts = []
            for at in (prow, urow):
                p = PM[j, at, :]
                edge = pltpu.roll(EM[at, :], LANES - (1, PAD, PAD + 1)[j], 1)
                pz = jnp.where(first, edge, pltpu.roll(p, 1, 1))
                parts.append((p + pz, pz - p))
            (s0, d0), (s1, d1) = parts
            lines.append((s0 + s1, s1 - s0, d0 + d1))
        for j in range(2):
            (ss0, ds0, sd0), (ss1, ds1, sd1) = lines[j], lines[j + 1]
            pressure = (ss0 - ss1, ds0 + ds1, sd0 + sd1)
            for r in range(3):
                at = 3 * j + r
                col = got if at == 0 else pltpu.roll(got, LANES - at, 1)
                total = FS[r, j, rows, :] + jnp.where(first, col, 0.0) - 0.2 * pressure[r]
                if j == 0:
                    total = total + SLR[r, rows, :]
                FS[r, j, rows, :] = total
        return 0

    lax.fori_loop(0, ym // ROWS, last_step, 0, unroll=4)
    f_out = local(FS, f_hbm)
    f_out.start()

    for cp in rates:
        cp.wait_send()
    sent(lo_x, hi_x, g, count)
    sent(lo_y, hi_y, h, n)
    sent(lo_f, hi_f, g, count)
    sent(lo_fy, hi_fy, h, n)

    @pl.when(h < n - 1)
    def _():
        rim.wait_send()

    for to, body, brim in mine:
        body.wait_send()

        @pl.when(to > 0)
        def _():
            brim.wait_send()

    @pl.when(has_hi)
    def _():
        slab.wait_send()
        for to, body, brim in ahead:
            body.wait_send()

            @pl.when(to > 0)
            def _():
                brim.wait_send()

    st_out.wait()
    pn_out.wait()
    f_out.wait()


def on_device(n, count, *args):
    strain_inc, pressure = args[0], args[5]
    planes, ym = strain_inc.shape[1], strain_inc.shape[2]
    ny = pressure.shape[1]
    assert ny <= LANES and ym % LANES == 0 and planes == 2 and strain_inc.shape[3] == LANES and pressure.shape[2] == n * LANES
    vm = lambda *shape: pltpu.VMEM(shape, F32)
    vi = lambda *shape: pltpu.VMEM(shape, jnp.int32)
    any_spec = pl.BlockSpec(memory_space=pl.ANY)
    smem = pl.BlockSpec(memory_space=pltpu.SMEM)
    loads = 3 * n + 7
    sends = (n - 1) + 10 + 2 * (n - 1) + 2 * n
    return pl.pallas_call(
        functools.partial(kernel, n, count),
        out_shape=(
            pltpu.VMEM(pressure.shape, F32),
            pltpu.VMEM(strain_inc.shape, F32),
            pltpu.VMEM((3,) + strain_inc.shape[1:], F32),
        ),
        in_specs=[any_spec, any_spec, any_spec, smem, smem, any_spec, any_spec, any_spec, smem],
        out_specs=(any_spec, any_spec, any_spec),
        scratch_shapes=[
            vm(6, 2, ym, LANES),
            vm(6, 2, ym, LANES),
            vi(2, ym, LANES),
            vm(2, ym, LANES),
            vm(n, 2, ny, LANES),
            vm(2, n, 2, ny + 2 * PAD, LANES),
            vi(n, 2, ny, LANES),
            vm(n, 2, ny, LANES),
            vm(2, 2, n, ny, LANES),
            vm(n, 2, ny + 2 * PAD, LANES),
            vm(2, n, ny, LANES),
            vm(6, n, 2, ny, LANES),
            vm(3, n, ny, LANES),
            vm(n, 2, ny, LANES),
            vm(n, ny, LANES),
            vm(n, PAD, LANES),
            vm(2, n, PAD, LANES),
            vm(3, PAD + ym, LANES),
            vm(PAD + ym, LANES),
            vm(6, 2, PAD + ym, LANES),
            vm(3, 2, ym, LANES),
            vm(3, ym, LANES),
            vm(3, ym, LANES),
            vm(ym, LANES),
            vm(ym, LANES),
            vm(16, ym),
            vm(16, ym),
            vm(2, ny, n * LANES),
            pltpu.SemaphoreType.DMA((loads,)),
            pltpu.SemaphoreType.DMA((sends,)),
            pltpu.SemaphoreType.DMA((sends,)),
        ],
        compiler_params=pltpu.CompilerParams(
            collective_id=0, has_side_effects=True, vmem_limit_bytes=56 * 1024 * 1024
        ),
    )(*args)


def solution(mesh):
    in_specs = (
        P(None, "gx", None, "gz"),
        P(None, "gx", None, "gz"),
        P("gx", None, "gz"),
        P(),
        P(),
        P("gx", "gz", None),
        P("gx", "gz", None),
        P("gx", "gz", None),
        P(),
    )
    out_specs = (P("gx", "gz", None), P(None, "gx", None, "gz"), P(None, "gx", None, "gz"))
    return jax.shard_map(
        functools.partial(on_device, mesh.shape["gz"], mesh.shape["gx"]),
        mesh=mesh,
        in_specs=in_specs,
        out_specs=out_specs,
        check_vma=False,
    )
```

```python
import functools

import jax
import jax.numpy as jnp
from jax import lax
from jax.experimental import pallas as pl
from jax.experimental.pallas import tpu as pltpu
from jax.sharding import PartitionSpec as P

MESH = pl.DeviceIdType.MESH
LANES = 128
PAD = 8
ROWS = 8
F32 = jnp.float32


def pick(ids, tables):
    levels = [list(t) for t in tables]
    bit = 1
    while len(levels[0]) > 1:
        odd = (ids & bit) != 0
        levels = [
            [jnp.where(odd, t[2 * j + 1], t[2 * j]) for j in range(len(t) // 2)] for t in levels
        ]
        bit *= 2
    return levels


def kernel(
    n,
    count,
    e_hbm,
    s_hbm,
    m_hbm,
    coh,
    fri,
    p_hbm,
    st_hbm,
    c_hbm,
    ptab,
    pn_hbm,
    so_hbm,
    f_hbm,
    E,
    S,
    M,
    SR,
    RF,
    PK,
    C,
    ST,
    HX,
    F1,
    HF,
    CO,
    CX,
    PN,
    EP,
    ET,
    ETR,
    PM,
    EM,
    T,
    FS,
    SL,
    SLR,
    RM,
    RMR,
    RT,
    RTR,
    OUTP,
    loc,
    snd,
    rcv,
):
    g = lax.axis_index("gx")
    h = lax.axis_index("gz")
    ym = SR.shape[1]
    ny = RF.shape[2]
    sem_at = [0, 0]
    rows_of = lambda who: pl.ds(pl.multiple_of(who * ny, 8), ny)
    prow_of = lambda who: pl.ds(pl.multiple_of(PAD + who * ny, 8), ny)

    def local(src, dst):
        k = sem_at[0]
        sem_at[0] += 1
        return pltpu.make_async_copy(src, dst, loc.at[k])

    def remote(src, dst, gx, gz):
        k = sem_at[1]
        sem_at[1] += 1
        return pltpu.make_async_remote_copy(
            src_ref=src,
            dst_ref=dst,
            send_sem=snd.at[k],
            recv_sem=rcv.at[k],
            device_id=(gx, gz),
            device_id_type=MESH,
        )

    has_lo, has_hi = g > 0, g < count - 1
    ld_p = [local(p_hbm.at[:, :, pl.ds(c * LANES, LANES)], PK.at[0, c, :, pl.ds(PAD, ny)]) for c in range(n)]
    ld_c = [local(c_hbm.at[:, :, pl.ds(c * LANES, LANES)], C.at[c]) for c in range(n)]
    ld_e = local(e_hbm.at[pl.ds(0, 3)], E.at[pl.ds(0, 3)])
    ld_e2 = local(e_hbm.at[pl.ds(3, 3)], E.at[pl.ds(3, 3)])
    ld_s = local(s_hbm, S)
    ld_m = local(m_hbm, M)
    ld_st = [local(st_hbm.at[:, :, pl.ds(c * LANES, LANES)], ST.at[c]) for c in range(n)]
    for cp in [ld_e] + ld_c + ld_p + [ld_m, ld_e2, ld_s] + ld_st:
        cp.start()

    PK[:, :, :, 0:PAD, :] = jnp.zeros((2, n, 2, PAD, LANES), F32)
    PK[:, :, :, PAD + ny : 2 * PAD + ny, :] = jnp.zeros((2, n, 2, PAD, LANES), F32)
    F1[:, :, 0:PAD, :] = jnp.zeros((n, 2, PAD, LANES), F32)
    F1[:, :, PAD + ny : 2 * PAD + ny, :] = jnp.zeros((n, 2, PAD, LANES), F32)

    @pl.when(jnp.logical_not(has_lo))
    def _():
        HX[0] = jnp.zeros(HX.shape[1:], F32)
        HF[0] = jnp.zeros(HF.shape[1:], F32)
        PM[0] = jnp.zeros(PM.shape[1:], F32)
        ETR[0] = jnp.zeros(ETR.shape[1:], F32)
        SLR[...] = jnp.zeros(SLR.shape, F32)

    @pl.when(jnp.logical_not(has_hi))
    def _():
        HX[1] = jnp.zeros(HX.shape[1:], F32)
        HF[1] = jnp.zeros(HF.shape[1:], F32)

    @pl.when(h == 0)
    def _():
        ETR[...] = jnp.zeros(ETR.shape, F32)
        RTR[...] = jnp.zeros(RTR.shape, F32)

    PM[:, 0:PAD, :] = jnp.zeros((3, PAD, LANES), F32)
    EM[0:PAD, :] = jnp.zeros((PAD, LANES), F32)
    T[:, :, 0:PAD, :] = jnp.zeros((6, 2, PAD, LANES), F32)

    barrier = pltpu.get_barrier_semaphore()
    for d in range(1, n):
        pl.semaphore_signal(barrier, inc=1, device_id=(g, lax.rem(h + d, n)), device_id_type=MESH)

    @pl.when(has_lo)
    def _():
        for d in range(n):
            pl.semaphore_signal(barrier, inc=1, device_id=(g - 1, lax.rem(h + d, n)), device_id_type=MESH)

    @pl.when(has_hi)
    def _():
        for d in range(n):
            pl.semaphore_signal(barrier, inc=1, device_id=(g + 1, lax.rem(h + d, n)), device_id_type=MESH)

    ld_e.wait()

    def rate_step(i, _):
        rows = pl.ds(pl.multiple_of(i * 16, 16), 16)
        SR[:, rows, :] = E[0, :, rows, :] + E[1, :, rows, :] + E[2, :, rows, :]
        return 0

    lax.fori_loop(0, ym // 16, rate_step, 0, unroll=8)
    for cp in ld_c:
        cp.wait()
    ptable = [ptab[j] for j in range(ptab.shape[0])]

    def cond_step(i, _):
        rows = pl.ds(pl.multiple_of(i * ROWS, ROWS), ROWS)
        for c in range(n):
            PK[1, c, :, pl.ds(pl.multiple_of(PAD + i * ROWS, ROWS), ROWS), :] = pick(
                C[c, :, rows, :], [ptable]
            )[0][0]
        return 0

    lax.fori_loop(0, ny // ROWS, cond_step, 0, unroll=min(8, ny // ROWS))
    for cp in ld_p:
        cp.wait()

    pl.semaphore_wait(barrier, (n - 1) + n * has_lo.astype(jnp.int32) + n * has_hi.astype(jnp.int32))

    rates = []
    for d in range(1, n):
        to = lax.rem(h + d, n)
        rates.append(remote(SR.at[:, rows_of(to), :], RF.at[h], g, to))
        rates[-1].start()
    both = pl.ds(0, 2)
    chunks = pl.ds(0, n)
    inner = pl.ds(PAD, ny)
    lo_x = remote(PK.at[both, chunks, 0, inner], HX.at[1], g - 1, h)
    hi_x = remote(PK.at[both, chunks, 1, inner], HX.at[0], g + 1, h)
    lo_y = remote(PK.at[:, :, :, pl.ds(PAD, PAD)], PK.at[:, :, :, pl.ds(PAD + ny, PAD)], g, h - 1)
    hi_y = remote(PK.at[:, :, :, pl.ds(ny, PAD)], PK.at[:, :, :, pl.ds(0, PAD)], g, h + 1)
    lo_f = remote(F1.at[chunks, 0, inner], HF.at[1], g - 1, h)
    hi_f = remote(F1.at[chunks, 1, inner], HF.at[0], g + 1, h)
    lo_fy = remote(F1.at[:, :, pl.ds(PAD, PAD)], F1.at[:, :, pl.ds(PAD + ny, PAD)], g, h - 1)
    hi_fy = remote(F1.at[:, :, pl.ds(ny, PAD)], F1.at[:, :, pl.ds(0, PAD)], g, h + 1)
    rim = remote(RT, RTR, g, h + 1)
    slab = remote(SL, SLR, g + 1, h)

    def begin(lo, hi, at, size):
        @pl.when(at > 0)
        def _():
            lo.start()

        @pl.when(at < size - 1)
        def _():
            hi.start()

    def arrive(lo, hi, at, size):
        @pl.when(at > 0)
        def _():
            hi.wait_recv()

        @pl.when(at < size - 1)
        def _():
            lo.wait_recv()

    def sent(lo, hi, at, size):
        @pl.when(at > 0)
        def _():
            lo.wait_send()

        @pl.when(at < size - 1)
        def _():
            hi.wait_send()

    begin(lo_x, hi_x, g, count)
    begin(lo_y, hi_y, h, n)
    RF[h] = SR[:, rows_of(h), :]

    ld_e2.wait()
    ld_s.wait()
    ld_m.wait()
    ctable = [coh[j] for j in range(coh.shape[0])]
    ftable = [fri[j] for j in range(fri.shape[0])]

    def plastic_step(i, _):
        rows = pl.ds(pl.multiple_of(i * ROWS, ROWS), ROWS)
        prow = pl.ds(pl.multiple_of(PAD + i * ROWS, ROWS), ROWS)
        vol = SR[:, rows, :]
        base = 1.5 * vol - 2.0 * (vol * (1.0 / 3.0))
        t = [S[c, :, rows, :] + 2.0 * E[c, :, rows, :] for c in range(6)]
        t = [t[0] + base, t[1] + base, t[2] + base] + t[3:]
        inv = t[0] + t[1] + t[2]
        third = inv * (1.0 / 3.0)
        dev = [t[0] - third, t[1] - third, t[2] - third] + t[3:]
        second = 0.5 * (dev[0] * dev[0] + dev[1] * dev[1] + dev[2] * dev[2])
        second = second + dev[3] * dev[3] + dev[4] * dev[4] + dev[5] * dev[5]
        q = jnp.sqrt(second)
        (strength,), (slope,) = pick(M[:, rows, :], [ctable, ftable])
        over = jnp.maximum(q + slope * inv - strength, 0.0)
        floor = jnp.maximum(q, 0.25)
        ratio = over / ((1.0 + 13.5 * slope * slope) * floor)
        shrink = jnp.maximum(1.0 - ratio, 0.0)
        mean = (inv - 13.5 * slope * (ratio * floor)) * (1.0 / 3.0)
        for c in range(6):
            out = dev[c] * shrink
            T[c, :, prow, :] = out + mean if c < 3 else out
        return 0

    lax.fori_loop(0, ym // ROWS, plastic_step, 0, unroll=8)
    st_out = local(T.at[:, :, pl.ds(PAD, ym)], so_hbm)
    st_out.start()

    lane = lax.broadcasted_iota(jnp.int32, (ROWS, LANES), 1)
    first = lane == 0
    final_lane = lane == LANES - 1
    zero = jnp.zeros((ROWS, LANES), F32)
    XC, YC, ZC = (0, 3, 5), (3, 1, 4), (5, 4, 2)

    def force_step(i, _):
        rows = pl.ds(pl.multiple_of(i * ROWS, ROWS), ROWS)
        prow = pl.ds(pl.multiple_of(PAD + i * ROWS, ROWS), ROWS)
        urow = pl.ds(PAD - 1 + i * ROWS, ROWS)
        main, side = [], []
        for a in range(2):
            s_now, d_now, s_up, d_up, r_now, r_up = [], [], [], [], [], []
            for c in range(6):
                t, u = T[c, a, prow, :], T[c, a, urow, :]
                tr, ur = pltpu.roll(t, 1, 1), pltpu.roll(u, 1, 1)
                tz, uz = jnp.where(first, 0.0, tr), jnp.where(first, 0.0, ur)
                s_now.append(t + tz)
                d_now.append(tz - t)
                s_up.append(u + uz)
                d_up.append(uz - u)
                r_now.append(tr)
                r_up.append(ur)
            line, edge = [], []
            for r in range(3):
                x, y, z = XC[r], YC[r], ZC[r]
                u_r = s_now[x] + s_up[x]
                v_r = (s_up[y] - s_now[y]) + (d_now[z] + d_up[z])
                line.append((0.25 * (v_r - u_r), 0.25 * (v_r + u_r)))
                u_r = r_now[x] + r_up[x]
                v_r = (r_up[y] - r_now[y]) + (r_now[z] + r_up[z])
                edge.append((0.25 * (v_r - u_r), 0.25 * (v_r + u_r)))
            main.append(line)
            side.append(edge)
        packed = zero
        for r in range(3):
            FS[r, 0, rows, :] = main[0][r][0]
            FS[r, 1, rows, :] = main[1][r][0] + main[0][r][1]
            SL[r, rows, :] = main[1][r][1]
            cols = [side[0][r][0], side[1][r][0] + side[0][r][1], side[1][r][1]]
            for j in range(3):
                at = 3 * j + r
                col = cols[j] if at == 0 else pltpu.roll(cols[j], at, 1)
                packed = jnp.where(lane == at, col, packed)
        RM[rows, :] = packed
        return 0

    lax.fori_loop(0, ym // ROWS, force_step, 0, unroll=8)

    for b in range(ym // LANES):
        block = slice(b * LANES, (b + 1) * LANES)
        RT[:, block] = jnp.transpose(RM[block, :])[0:16]

    @pl.when(h < n - 1)
    def _():
        rim.start()

    for cp in ld_st:
        cp.wait()
    for cp in rates:
        cp.wait_recv()
    arrive(lo_x, hi_x, g, count)
    arrive(lo_y, hi_y, h, n)

    def up_one(parts):
        turned = [pltpu.roll(x, LANES - 1, 1) for x in parts]
        return [jnp.where(final_lane, turned[c + 1] if c + 1 < n else 0.0, turned[c]) for c in range(n)]

    def down_one(parts):
        turned = [pltpu.roll(x, 1, 1) for x in parts]
        return [jnp.where(first, turned[c - 1] if c > 0 else 0.0, turned[c]) for c in range(n)]

    def face(a, b):
        return 2.0 * a * b / (a + b)

    def sweep_one(i, _):
        rows = pl.ds(pl.multiple_of(i * ROWS, ROWS), ROWS)
        prow = pl.ds(pl.multiple_of(PAD + i * ROWS, ROWS), ROWS)
        urow = pl.ds(PAD - 1 + i * ROWS, ROWS)
        drow = pl.ds(PAD + 1 + i * ROWS, ROWS)
        mids = []
        for a in range(2):
            k = [PK[1, c, a, prow, :] for c in range(n)]
            p = [PK[0, c, a, prow, :] for c in range(n)]
            tzp = [face(x, y) for x, y in zip(k, up_one(k))]
            tzm = down_one(tzp)
            pzp, pzm = up_one(p), down_one(p)
            for c in range(n):
                tym = face(k[c], PK[1, c, a, urow, :])
                typ = face(k[c], PK[1, c, a, drow, :])
                out = face(k[c], HX[a, 1, c, rows, :])
                if a == 0:
                    mids.append(face(k[c], PK[1, c, 1, prow, :]))
                    CX[0, c, rows, :] = mids[c]
                CX[1 + a, c, rows, :] = out
                st = ST[c, a, rows, :]
                source = st * p[c] - 0.8 * RF[c, a, rows, :]
                inverse = 1.0 / (st + out + mids[c] + tym + typ + tzm[c] + tzp[c])
                num = (
                    source
                    + out * HX[a, 0, c, rows, :]
                    + mids[c] * PK[0, c, 1 - a, prow, :]
                    + tym * PK[0, c, a, urow, :]
                    + typ * PK[0, c, a, drow, :]
                    + tzm[c] * pzm[c]
                    + tzp[c] * pzp[c]
                )
                for j, val in enumerate((tym, typ, tzm[c], tzp[c], inverse, source)):
                    CO[j, c, a, rows, :] = val
                F1[c, a, prow, :] = num * inverse
        return 0

    lax.fori_loop(0, ny // ROWS, sweep_one, 0, unroll=min(8, ny // ROWS))
    begin(lo_f, hi_f, g, count)
    begin(lo_fy, hi_fy, h, n)

    @pl.when(h > 0)
    def _():
        rim.wait_recv()

    for b in range(ym // LANES):
        block = slice(b * LANES, (b + 1) * LANES)
        RMR[block, :] = jnp.transpose(
            jnp.concatenate([RTR[:, block], jnp.zeros((LANES - 16, LANES), F32)], axis=0)
        )

    def slab_step(i, _):
        rows = pl.ds(pl.multiple_of(i * ROWS, ROWS), ROWS)
        got = RMR[rows, :]
        for r in range(3):
            SL[r, rows, :] = SL[r, rows, :] + jnp.where(first, pltpu.roll(got, LANES - 6 - r, 1), 0.0)
        return 0

    lax.fori_loop(0, ym // ROWS, slab_step, 0, unroll=8)

    arrive(lo_f, hi_f, g, count)
    arrive(lo_fy, hi_fy, h, n)

    def sweep_two(i, _):
        rows = pl.ds(pl.multiple_of(i * ROWS, ROWS), ROWS)
        prow = pl.ds(pl.multiple_of(PAD + i * ROWS, ROWS), ROWS)
        urow = pl.ds(PAD - 1 + i * ROWS, ROWS)
        drow = pl.ds(PAD + 1 + i * ROWS, ROWS)
        result = []
        for a in range(2):
            p = [F1[c, a, prow, :] for c in range(n)]
            pzp, pzm = up_one(p), down_one(p)
            line = []
            for c in range(n):
                tym, typ, tzm, tzp, inverse, source = (CO[j, c, a, rows, :] for j in range(6))
                num = (
                    source
                    + CX[1 + a, c, rows, :] * HF[a, c, rows, :]
                    + CX[0, c, rows, :] * F1[c, 1 - a, prow, :]
                    + tym * F1[c, a, urow, :]
                    + typ * F1[c, a, drow, :]
                    + tzm * pzm[c]
                    + tzp * pzp[c]
                )
                new = num * inverse
                PN[c, a, rows, :] = new
                OUTP[a, rows, pl.ds(c * LANES, LANES)] = new
                line.append(new)
            result.append(line)
        for c in range(1, n):
            left, right = pltpu.roll(result[0][c - 1], 1, 1), pltpu.roll(result[1][c - 1], 2, 1)
            EP[c, rows, :] = jnp.where(first, left, right)
        return 0

    lax.fori_loop(0, ny // ROWS, sweep_two, 0, unroll=min(8, ny // ROWS))

    for c in range(1, n):
        cols = EP[c]
        if ny < LANES:
            cols = jnp.concatenate([cols, jnp.zeros((LANES - ny, LANES), F32)], axis=0)
        ET[c] = jnp.transpose(cols)[0:PAD]

    mine, ahead = [], []
    for d in range(1, n):
        to = lax.rem(h + d, n)
        mine.append((to, remote(PN.at[to], PM.at[pl.ds(1, 2), prow_of(h)], g, to), remote(ET.at[to], ETR.at[1, h], g, to)))
    for d in range(n):
        to = lax.rem(h + d, n)
        ahead.append((to, remote(PN.at[to, 1], PM.at[0, prow_of(h)], g + 1, to), remote(ET.at[to], ETR.at[0, h], g + 1, to)))
    for to, body, brim in mine:
        body.start()

        @pl.when(to > 0)
        def _():
            brim.start()

    @pl.when(has_hi)
    def _():
        for to, body, brim in ahead:
            body.start()

            @pl.when(to > 0)
            def _():
                brim.start()

    @pl.when(has_hi)
    def _():
        slab.start()

    pn_out = local(OUTP, pn_hbm)
    pn_out.start()
    PM[1:3, prow_of(h), :] = PN[h]

    @pl.when(h > 0)
    def _():
        ETR[1, h] = ET[h]

    @pl.when(has_lo)
    def _():
        slab.wait_recv()

    for to, body, brim in mine:
        body.wait_recv()

        @pl.when(h > 0)
        def _():
            brim.wait_recv()

    @pl.when(has_lo)
    def _():
        for to, body, brim in ahead:
            body.wait_recv()

            @pl.when(h > 0)
            def _():
                brim.wait_recv()

    for c in range(n):
        parts = [ETR[0, c], ETR[1, c], jnp.zeros((LANES - 2 * PAD, LANES), F32)]
        EM[PAD + c * ny : PAD + (c + 1) * ny, :] = jnp.transpose(
            jnp.concatenate(parts, axis=0)
        )[0:ny]

    def last_step(i, _):
        rows = pl.ds(pl.multiple_of(i * ROWS, ROWS), ROWS)
        prow = pl.ds(pl.multiple_of(PAD + i * ROWS, ROWS), ROWS)
        urow = pl.ds(PAD - 1 + i * ROWS, ROWS)
        got = RMR[rows, :]
        lines = []
        for j in range(3):
            parts = []
            for at in (prow, urow):
                p = PM[j, at, :]
                edge = pltpu.roll(EM[at, :], LANES - (1, PAD, PAD + 1)[j], 1)
                pz = jnp.where(first, edge, pltpu.roll(p, 1, 1))
                parts.append((p + pz, pz - p))
            (s0, d0), (s1, d1) = parts
            lines.append((s0 + s1, s1 - s0, d0 + d1))
        for j in range(2):
            (ss0, ds0, sd0), (ss1, ds1, sd1) = lines[j], lines[j + 1]
            pressure = (ss0 - ss1, ds0 + ds1, sd0 + sd1)
            for r in range(3):
                at = 3 * j + r
                col = got if at == 0 else pltpu.roll(got, LANES - at, 1)
                total = FS[r, j, rows, :] + jnp.where(first, col, 0.0) - 0.2 * pressure[r]
                if j == 0:
                    total = total + SLR[r, rows, :]
                FS[r, j, rows, :] = total
        return 0

    lax.fori_loop(0, ym // ROWS, last_step, 0, unroll=8)
    f_out = local(FS, f_hbm)
    f_out.start()

    for cp in rates:
        cp.wait_send()
    sent(lo_x, hi_x, g, count)
    sent(lo_y, hi_y, h, n)
    sent(lo_f, hi_f, g, count)
    sent(lo_fy, hi_fy, h, n)

    @pl.when(h < n - 1)
    def _():
        rim.wait_send()

    for to, body, brim in mine:
        body.wait_send()

        @pl.when(to > 0)
        def _():
            brim.wait_send()

    @pl.when(has_hi)
    def _():
        slab.wait_send()
        for to, body, brim in ahead:
            body.wait_send()

            @pl.when(to > 0)
            def _():
                brim.wait_send()

    st_out.wait()
    pn_out.wait()
    f_out.wait()


def on_device(n, count, *args):
    strain_inc, pressure = args[0], args[5]
    planes, ym = strain_inc.shape[1], strain_inc.shape[2]
    ny = pressure.shape[1]
    assert ny <= LANES and ym % LANES == 0 and planes == 2 and strain_inc.shape[3] == LANES and pressure.shape[2] == n * LANES
    vm = lambda *shape: pltpu.VMEM(shape, F32)
    vi = lambda *shape: pltpu.VMEM(shape, jnp.int32)
    any_spec = pl.BlockSpec(memory_space=pl.ANY)
    smem = pl.BlockSpec(memory_space=pltpu.SMEM)
    loads = 3 * n + 7
    sends = (n - 1) + 10 + 2 * (n - 1) + 2 * n
    return pl.pallas_call(
        functools.partial(kernel, n, count),
        out_shape=(
            pltpu.VMEM(pressure.shape, F32),
            pltpu.VMEM(strain_inc.shape, F32),
            pltpu.VMEM((3,) + strain_inc.shape[1:], F32),
        ),
        in_specs=[any_spec, any_spec, any_spec, smem, smem, any_spec, any_spec, any_spec, smem],
        out_specs=(any_spec, any_spec, any_spec),
        scratch_shapes=[
            vm(6, 2, ym, LANES),
            vm(6, 2, ym, LANES),
            vi(2, ym, LANES),
            vm(2, ym, LANES),
            vm(n, 2, ny, LANES),
            vm(2, n, 2, ny + 2 * PAD, LANES),
            vi(n, 2, ny, LANES),
            vm(n, 2, ny, LANES),
            vm(2, 2, n, ny, LANES),
            vm(n, 2, ny + 2 * PAD, LANES),
            vm(2, n, ny, LANES),
            vm(6, n, 2, ny, LANES),
            vm(3, n, ny, LANES),
            vm(n, 2, ny, LANES),
            vm(n, ny, LANES),
            vm(n, PAD, LANES),
            vm(2, n, PAD, LANES),
            vm(3, PAD + ym, LANES),
            vm(PAD + ym, LANES),
            vm(6, 2, PAD + ym, LANES),
            vm(3, 2, ym, LANES),
            vm(3, ym, LANES),
            vm(3, ym, LANES),
            vm(ym, LANES),
            vm(ym, LANES),
            vm(16, ym),
            vm(16, ym),
            vm(2, ny, n * LANES),
            pltpu.SemaphoreType.DMA((loads,)),
            pltpu.SemaphoreType.DMA((sends,)),
            pltpu.SemaphoreType.DMA((sends,)),
        ],
        compiler_params=pltpu.CompilerParams(
            collective_id=0, has_side_effects=True, vmem_limit_bytes=56 * 1024 * 1024
        ),
    )(*args)


def solution(mesh):
    in_specs = (
        P(None, "gx", None, "gz"),
        P(None, "gx", None, "gz"),
        P("gx", None, "gz"),
        P(),
        P(),
        P("gx", "gz", None),
        P("gx", "gz", None),
        P("gx", "gz", None),
        P(),
    )
    out_specs = (P("gx", "gz", None), P(None, "gx", None, "gz"), P(None, "gx", None, "gz"))
    return jax.shard_map(
        functools.partial(on_device, mesh.shape["gz"], mesh.shape["gx"]),
        mesh=mesh,
        in_specs=in_specs,
        out_specs=out_specs,
        check_vma=False,
    )
```
